256 devices in a mesh: replica: 8 (over x_hi, y), shard: 32 (over x_lo, z, core).
Axes of the slice: x: 4 (x_hi: 2, x_lo: 2; x = x_hi * 2 + x_lo), y: 4, z: 8, core: 2. Of those that a mesh axis runs over, the one named last changes fastest.
Arguments:
- tokens: bfloat16 [32768, 8192], P(('replica', 'shard')), may hold values from -24 to 24
- cotangent: bfloat16 [32768, 512], P(('replica', 'shard')), may hold values from -6 to 6
- base_copy: bfloat16 [8192, 512], replicated, may hold values from -0.0625 to 0.0625
- codes: int32 [8192, 512], P('shard'), may hold values from -8 to 7
- scales: float32 [8192, 4], P('shard'), may hold values from 0.001 to 0.004
Outputs:
- projected: bfloat16 [32768, 512], P(('replica', 'shard'))
- input_grad: bfloat16 [32768, 8192], P(('replica', 'shard'))
- weight_grad: float32 [8192, 512], P('shard')
The draws below stay inside these ranges and needn't reach their ends.
All inputs are finite; a program needn't handle non-finite values.
Results may differ from the reference program's by a relative error of at most 0.0055.
Values may be sent and summed in bfloat16 or wider, within the bound.
A program may use at most 128 MiB of HBM per device.

```python
import math
import jax
import jax.numpy as jnp
from jax import lax

D = 8192
KVW = 512
GROUP = 128
TOKENS = 32768


def with_ends(drawn, key, smallest, largest):
    dims = drawn.shape
    spot = [jax.random.randint(jax.random.fold_in(key, axis), (), 0, dims[axis]) for axis in range(len(dims))]
    drawn = drawn.at[tuple(spot)].set(smallest)
    longest = dims.index(max(dims))
    spot[longest] = (spot[longest] + 1) % dims[longest]
    return drawn.at[tuple(spot)].set(largest)


def raised(drawn, own_key, source, target, blocks, factor):
    def block_of(axis_at):
        return (jnp.arange(drawn.shape[axis_at]) // (drawn.shape[axis_at] // blocks)).reshape((-1,) + (1,) * (drawn.ndim - 1 - axis_at))

    one_side = jax.random.permutation(own_key, blocks)[block_of(target)]
    far = (block_of(target) + blocks // 2) % blocks
    return jnp.where((block_of(source) == one_side) | (block_of(source) == far), factor * drawn, drawn)


def level_of(own_key, extent, cuts, low, high):
    def one(dim, parts):
        heights = jax.random.uniform(jax.random.fold_in(jax.random.fold_in(own_key, 6), dim), (parts,), jnp.float32, low / len(cuts), high / len(cuts))
        return jnp.repeat(jnp.exp(heights), extent[dim] // parts).reshape((-1,) + (1,) * (len(extent) - dim - 1))

    factor_of = one(*cuts[0])
    for cut in cuts[1:]:
        factor_of = factor_of * one(*cut)
    return factor_of


def bell_draw(rng, extent, spread, limit, cuts=(), held_as=jnp.bfloat16):
    gain = level_of(rng, extent, cuts, -0.22, 0.18) if cuts else 1.0
    array = jax.random.normal(rng, extent, jnp.float32) * spread * gain
    return jnp.minimum(jnp.maximum(array, -limit), limit).astype(held_as)


def bell_draw_with(stream_key, shape, scale, bound, shards, heavy, dtype=jnp.bfloat16):
    entries = scale * jax.random.normal(stream_key, shape, jnp.float32)
    if shards:
        entries = entries * level_of(stream_key, shape, shards, -0.22, 0.18)
    return jnp.clip(raised(entries, jax.random.fold_in(stream_key, 3), *heavy), -bound, bound).astype(dtype)


def setup_inputs(seed: int = 0) -> dict:
    arg_keys = jax.random.split(jax.random.key(seed), 6)
    return {
        "tokens": bell_draw_with(arg_keys[0], (TOKENS, D), 1.0, 24.0, ((0, 256),), (0, 1, 256, 6.0)),
        "cotangent": bell_draw(arg_keys[1], (TOKENS, KVW), 1.0, 6.0, ((0, 256),)),
        "base_copy": bell_draw(arg_keys[2], (D, KVW), D ** -0.5, 0.0625),
        "codes": with_ends(jax.random.randint(arg_keys[3], (D, KVW), -8, 8), jax.random.fold_in(arg_keys[3], 1), -8, 7).astype(jnp.int32),
        "scales": jnp.clip(jnp.exp(math.log(0.004) - 1.3862944 * jax.random.uniform(arg_keys[4], (D, KVW // GROUP), jnp.float32) ** level_of(arg_keys[4], (D, KVW // GROUP), ((0, 32),), -0.2, 0.2)), 0.001, 0.004),
    }


def reference(tokens, cotangent, base_copy, codes, scales):
    rows, width = codes.shape
    difference = (codes.astype(jnp.float32).reshape(rows, width // GROUP, GROUP) * scales[:, :, None]).reshape(rows, width).astype(jnp.bfloat16)
    weight = (base_copy.astype(jnp.float32) + difference.astype(jnp.float32)).astype(jnp.bfloat16)
    projected = jnp.dot(tokens, weight, preferred_element_type=jnp.float32).astype(jnp.bfloat16)
    input_grad = jnp.dot(cotangent, weight.T, preferred_element_type=jnp.float32).astype(jnp.bfloat16)
    factor = 1.0 / math.sqrt(TOKENS)
    weight_grad = lax.dot_general(tokens, cotangent, (((0,), (0,)), ((), ())), preferred_element_type=jnp.float32) * factor
    return (projected, input_grad, weight_grad)
```

```python
import math

import jax
import jax.numpy as jnp
from jax import lax
from jax.experimental import pallas as pl
from jax.experimental.pallas import tpu as pltpu
from jax.sharding import PartitionSpec as P

BF16 = jnp.bfloat16
F32 = jnp.float32


def kernel(
    tok, cot, base, codes, scales,
    proj, igrad, wgrad,
    W, BASE, TK, CA, TW, GF, GX, XR, ZS, ZR, RB, RR, IG, PA, PR, CO, SC,
    ld, tk_l, tk_s, tk_r, ca_s, ca_r, tw_s, tw_r, az_s, az_r, ax_s, ax_r,
    ig_l, ig_s, ig_r, gx_s, gx_r, zs_s, zs_r, rr_s, rr_r, pa_s, pa_r,
):
    r = lax.axis_index("replica")
    s = lax.axis_index("shard")
    X, y = r // 4, r % 4
    l, z, c = s // 16, (s % 16) // 2, s % 2
    oc = 1 - c

    def dev(X=X, y=y, l=l, z=z, c=c):
        return {"replica": X * 4 + y, "shard": l * 16 + z * 2 + c}

    up, down = dev(z=(z + 1) % 8), dev(z=(z + 7) % 8)
    A, B, O = dev(l=1 - l), dev(X=1 - X, l=1 - l), dev(X=1 - X)
    peer = dev(c=oc)

    def wait(ref, sem):
        pltpu.make_async_copy(ref, ref, sem).wait()

    def send(src, dst, ssem, rsem, to):
        pltpu.make_async_remote_copy(src, dst, ssem, rsem, device_id=to).start()

    pltpu.make_async_copy(codes, CO, ld.at[0]).start()
    pltpu.make_async_copy(scales, SC, ld.at[1]).start()
    me8 = y * 2 + c
    pltpu.make_async_copy(cot, CA.at[me8], ca_r.at[me8]).start()

    barrier = pltpu.get_barrier_semaphore()
    peers = [peer]
    peers += [dev(y=(y + d) % 4, c=cc) for d in (1, 2, 3) for cc in (c, oc)]
    peers += [dev(z=(z + d) % 8) for d in range(1, 8)]
    peers += [A, B, O]
    peers += [dev(X=1 - X, y=(y + d) % 4) for d in (1, 2, 3)]
    for d in peers:
        pl.semaphore_signal(barrier, 1, device_id=d)

    def col(block, core):
        return pl.multiple_of((block * 2 + core) * 256, 256)

    def load_block(b, _):
        rows = pl.ds(col(b, c), 256)
        pltpu.make_async_copy(base.at[rows], BASE.at[b], ld.at[2]).start()
        dst = pl.ds(pl.multiple_of(b * 256, 256), 256)
        pltpu.make_async_copy(
            tok.at[:, rows], TK.at[pl.ds(c * 128, 128), dst], tk_l
        ).start()
        return 0

    lax.fori_loop(0, 16, load_block, 0)

    wait(CO, ld.at[0])
    wait(SC, ld.at[1])
    own = l * 8 + z
    for g in range(4):
        lanes = pl.ds(g * 128, 128)
        W[own, :, lanes] = (CO[:, lanes].astype(F32) * SC[:, g : g + 1]).astype(BF16)

    pl.semaphore_wait(barrier, len(peers))

    def half(block, h):
        return W.at[block, pl.ds(h * 128, 128)]

    def send_z(block, t, way, h):
        send(half(block, h), half(block, h), az_s, az_r.at[t, way, h], (up, down)[way])

    def send_x(block, zz, h):
        send(half(block, h), half(block, h), ax_s, ax_r.at[zz, h], (A, B)[h])

    for h in range(2):
        send_z(own, 0, 0, h)
        send_z(own, 0, 1, h)
        send_x(own, z, h)

    send(cot, CA.at[me8], ca_s, ca_r.at[me8], peer)
    for d in (1, 3, 2):
        send(cot, CA.at[me8], ca_s, ca_r.at[me8], dev(y=(y + d) % 4))

    def send_tokens(b, _):
        src = pl.ds(col(b, oc), 256)
        dst = pl.ds(pl.multiple_of(b * 256, 256), 256)
        send(tok.at[:, src], TK.at[pl.ds(c * 128, 128), dst], tk_s, tk_r, peer)
        return 0

    lax.fori_loop(0, 16, send_tokens, 0)

    my_rows = pl.ds(pl.multiple_of(me8 * 128, 128), 128)

    def kof(i):
        return lax.rem(z // 2 + i + 1, 4)

    def chunk(p, i, j, core):
        return pl.multiple_of(
            ((p * 8 + 2 * kof(i) + j % 2) * 2 + core) * 256 + (j // 2) * 128, 128
        )

    def send_part(i):
        for p in range(2):
            dst = TW.at[i, my_rows, pl.ds(p * 128, 128)]
            pltpu.make_async_copy(
                tok.at[:, pl.ds(chunk(p, i, y, c), 128)], dst, tw_r.at[i]
            ).start()
            for d in (1, 3, 2, 0):
                j = (y + d) % 4
                for cc in (c, oc):
                    if d == 0 and cc is c:
                        continue
                    send(
                        tok.at[:, pl.ds(chunk(p, i, j, cc), 128)], dst, tw_s, tw_r.at[i],
                        dev(y=j, c=cc),
                    )

    send_part(0)
    send_part(1)

    PA[...] = jnp.zeros_like(PA)
    wait(CA.at[me8], ca_r.at[me8])
    wait(CA.at[y * 2 + oc], ca_r.at[y * 2 + oc])
    wait(BASE, ld.at[2])
    half_tokens = TK.at[pl.ds(0, 128)]
    wait(half_tokens, tk_l)
    wait(half_tokens, tk_r)

    def offset(m):
        return jnp.where(m % 2 == 1, 8 - (m + 1) // 2, m // 2)

    def use_block(other, m):
        zz = lax.rem(z + offset(m), 8)
        block = jnp.where(other, (1 - l) * 8 + zz, l * 8 + zz)

        @pl.when(other)
        def _():
            for h in range(2):
                wait(half(block, h), ax_r.at[zz, h])

        w = (BASE[block].astype(F32) + W[block].astype(F32)).astype(BF16)
        lanes = pl.ds(pl.multiple_of(block * 256, 256), 256)
        PA[...] += jnp.dot(TK[:, lanes], w, preferred_element_type=F32)
        both = CA[pl.ds(y * 2, 2)].reshape(256, 512)
        IG[block] = lax.dot_general(
            both, w, (((1,), (1,)), ((), ())), preferred_element_type=F32
        ).astype(BF16)
        out = igrad.at[:, pl.ds(col(block, c), 256)]
        mine = IG.at[block, pl.ds(pl.multiple_of(c * 128, 128), 128)]
        theirs = IG.at[block, pl.ds(pl.multiple_of(oc * 128, 128), 128)]
        send(theirs, out, ig_s, ig_r, peer)
        pltpu.make_async_copy(mine, out, ig_l).start()

    def piece(p, half_x):
        return pl.multiple_of(p * 128 + half_x * 64, 64)

    def x_sum(i):
        wait(XR.at[i], gx_r.at[i])
        total = GF[pl.ds(piece(l, X), 64), :]
        for q in range(3):
            total = total + XR[i, q].astype(F32)
        ZS[i] = total.astype(BF16)
        to = 2 * kof(i) + y % 2

        @pl.when(to != z)
        def _():
            send(ZS.at[i], ZR.at[z], zs_s, zs_r, dev(z=to))

        @pl.when(to == z)
        def _():
            ZR[z] = total.astype(BF16)

    def part(i):
        @pl.when(i == 0)
        def _():
            for d in (1, 3, 2):
                k = ((y + d) % 4) * 2 + c
                wait(CA.at[k], ca_r.at[k])
                send(CA.at[k], CA.at[k], ca_s, ca_r.at[k], peer)
            for d in (1, 3, 2):
                k = ((y + d) % 4) * 2 + oc
                wait(CA.at[k], ca_r.at[k])

        wait(TW.at[i], tw_r.at[i])
        GF[...] = lax.dot_general(
            TW[i], CA[...].reshape(1024, 512), (((0,), (0,)), ((), ())),
            preferred_element_type=F32,
        )
        GX[i] = GF[...].astype(BF16)
        for q, (p, hx, to) in enumerate(((1 - l, X, A), (1 - l, 1 - X, B), (l, 1 - X, O))):
            send(GX.at[i, pl.ds(piece(p, hx), 64)], XR.at[i, q], gx_s, gx_r.at[i], to)

    def step(i, _):
        @pl.when(i < 4)
        def _():
            t = i
            zu, zd = lax.rem(z + 7 - t, 8), lax.rem(z + t + 1, 8)
            for h in range(2):
                for way, zz in ((0, zu), (1, zd)):
                    block = l * 8 + zz

                    @pl.when(jnp.logical_or(t < 3, h == way))
                    def _():
                        wait(half(block, h), az_r.at[t, way, h])

                        @pl.when(jnp.logical_or(t < 2, jnp.logical_and(t == 2, h == way)))
                        def _():
                            send_z(block, t + 1, way, h)

                        send_x(block, zz, h)

        @pl.when(i < 2)
        def _():
            send_part(i + 2)

        lo1 = jnp.where(i == 0, 0, jnp.minimum(2 * i + 1, 8))
        hi1 = jnp.minimum(2 * i + 3, 8)
        lo2 = jnp.maximum(2 * i - 1, 0)
        hi2 = jnp.minimum(2 * i + 1, 8)
        n1 = hi1 - lo1

        def one(n, _):
            other = n >= n1
            use_block(other, jnp.where(other, lo2 + n - n1, lo1 + n))
            return 0

        lax.fori_loop(0, n1 + hi2 - lo2, one, 0)

        @pl.when(i == 4)
        def _():
            send(PA.at[pl.ds(pl.multiple_of(oc * 128, 128), 128)], PR, pa_s, pa_r, peer)

        @pl.when(i > 0)
        def _():
            x_sum(i - 1)

        @pl.when(i < 4)
        def _():
            part(i)

        return 0

    lax.fori_loop(0, 5, step, 0)

    holds = z % 2 == y % 2
    slot = (y // 2) * 2 + X

    @pl.when(holds)
    def _():
        wait(ZR.at[pl.ds(0, 7)], zs_r)
        total = ZR[0].astype(F32)
        for q in range(1, 8):
            total = total + ZR[q].astype(F32)
        total = (total * (1.0 / math.sqrt(32768.0))).astype(BF16)
        RB[...] = total
        for XX in (X, 1 - X):
            for d in (1, 2, 3, 0):
                if XX is X and d == 0:
                    continue
                send(RB, RR.at[slot], rr_s, rr_r, dev(X=XX, y=(y + d) % 4))
        RR[slot] = total

    wait(PR, pa_r)
    proj[...] = (PA[pl.ds(pl.multiple_of(c * 128, 128), 128), :] + PR[...]).astype(BF16)

    @pl.when(holds)
    def _():
        wait(RR.at[pl.ds(0, 3)], rr_r)

    @pl.when(jnp.logical_not(holds))
    def _():
        wait(RR, rr_r)

    for q in range(4):
        wgrad[pl.ds(q * 64, 64), :] = RR[q].astype(F32)

    wait(half_tokens, tk_s)
    wait(CA.at[pl.ds(0, 7)], ca_s)
    wait(TW.at[:, pl.ds(0, 896)], tw_s)
    wait(W.at[pl.ds(0, 7)], az_s)
    wait(W.at[pl.ds(0, 8)], ax_s)
    wait(XR, gx_s)
    wait(PR, pa_s)

    @pl.when(holds)
    def _():
        wait(ZS.at[pl.ds(0, 3)], zs_s)
        wait(ZR.at[pl.ds(0, 7)], rr_s)

    @pl.when(jnp.logical_not(holds))
    def _():
        wait(ZS, zs_s)

    wait(half_tokens, ig_s)
    wait(half_tokens, ig_l)
    wait(half_tokens, ig_r)


def body(tokens, cotangent, base_copy, codes, scales):
    dma = pltpu.SemaphoreType.DMA
    anywhere = pl.BlockSpec(memory_space=pl.ANY)
    return pl.pallas_call(
        kernel,
        out_shape=(
            jax.ShapeDtypeStruct((128, 512), BF16),
            jax.ShapeDtypeStruct((128, 8192), BF16),
            jax.ShapeDtypeStruct((256, 512), F32),
        ),
        in_specs=[anywhere] * 5,
        out_specs=(
            pl.BlockSpec(memory_space=pltpu.VMEM),
            anywhere,
            pl.BlockSpec(memory_space=pltpu.VMEM),
        ),
        scratch_shapes=[
            pltpu.VMEM((16, 256, 512), BF16),
            pltpu.VMEM((16, 256, 512), BF16),
            pltpu.VMEM((256, 4096), BF16),
            pltpu.VMEM((8, 128, 512), BF16),
            pltpu.VMEM((4, 1024, 256), BF16),
            pltpu.VMEM((256, 512), F32),
            pltpu.VMEM((4, 256, 512), BF16),
            pltpu.VMEM((4, 3, 64, 512), BF16),
            pltpu.VMEM((4, 64, 512), BF16),
            pltpu.VMEM((8, 64, 512), BF16),
            pltpu.VMEM((64, 512), BF16),
            pltpu.VMEM((4, 64, 512), BF16),
            pltpu.VMEM((16, 256, 256), BF16),
            pltpu.VMEM((256, 512), F32),
            pltpu.VMEM((128, 512), F32),
            pltpu.VMEM((256, 512), jnp.int32),
            pltpu.VMEM((256, 4), F32),
            dma((3,)),
            dma, dma, dma,
            dma, dma((8,)),
            dma, dma((4,)),
            dma, dma((4, 2, 2)),
            dma, dma((8, 2)),
            dma, dma, dma,
            dma, dma((4,)),
            dma, dma,
            dma, dma,
            dma, dma,
        ],
        compiler_params=pltpu.CompilerParams(
            collective_id=0, has_side_effects=True, vmem_limit_bytes=48 << 20
        ),
        cost_estimate=pl.CostEstimate(
            flops=6 * 128 * 8192 * 512, bytes_accessed=24 << 20, transcendentals=0
        ),
    )(tokens, cotangent, base_copy, codes, scales)


def solution(mesh):
    return jax.shard_map(
        body,
        mesh=mesh,
        in_specs=(
            P(("replica", "shard"), None),
            P(("replica", "shard"), None),
            P(),
            P("shard", None),
            P("shard", None),
        ),
        out_specs=(P(("replica", "shard"), None), P(("replica", "shard"), None), P("shard", None)),
        check_vma=False,
    )
```

```python
import math

import jax
import jax.numpy as jnp
from jax import lax
from jax.experimental import pallas as pl
from jax.experimental.pallas import tpu as pltpu
from jax.sharding import PartitionSpec as P

BF16 = jnp.bfloat16
F32 = jnp.float32


def kernel(
    tok, cot, base, codes, scales,
    proj, igrad, wgrad,
    W, BASE, TK, CA, TW, GF, GX, XR, ZS, ZR, RB, RR, IG, PA, PR, CO, SC,
    ld, tk_l, tk_s, tk_r, ca_s, ca_r, tw_s, tw_r, az_s, az_r, bz_s, bz_r, ao_s, ax_s, ax_r,
    ig_l, ig_s, ig_r, gx_s, gx_r, zs_s, zs_r, rr_s, rr_r, pa_s, pa_r,
):
    r = lax.axis_index("replica")
    s = lax.axis_index("shard")
    X, y = r // 4, r % 4
    l, z, c = s // 16, (s % 16) // 2, s % 2
    oc = 1 - c

    def dev(X=X, y=y, l=l, z=z, c=c):
        return {"replica": X * 4 + y, "shard": l * 16 + z * 2 + c}

    up, down = dev(z=(z + 1) % 8), dev(z=(z + 7) % 8)
    A, B, O = dev(l=1 - l), dev(X=1 - X, l=1 - l), dev(X=1 - X)
    peer = dev(c=oc)

    def wait(ref, sem):
        pltpu.make_async_copy(ref, ref, sem).wait()

    def send(src, dst, ssem, rsem, to):
        pltpu.make_async_remote_copy(src, dst, ssem, rsem, device_id=to).start()

    pltpu.make_async_copy(codes, CO, ld.at[0]).start()
    pltpu.make_async_copy(scales, SC, ld.at[1]).start()
    me8 = y * 2 + c
    pltpu.make_async_copy(cot, CA.at[me8], ca_r.at[me8]).start()

    barrier = pltpu.get_barrier_semaphore()
    peers = [peer]
    peers += [dev(y=(y + d) % 4, c=cc) for d in (1, 2, 3) for cc in (c, oc)]
    peers += [dev(z=(z + d) % 8) for d in range(1, 8)]
    peers += [A, B, O]
    peers += [dev(X=1 - X, y=(y + d) % 4) for d in (1, 2, 3)]
    for d in peers:
        pl.semaphore_signal(barrier, 1, device_id=d)

    def col(block, core):
        return pl.multiple_of((block * 2 + core) * 256, 256)

    def load_block(b, _):
        rows = pl.ds(col(b, c), 256)
        pltpu.make_async_copy(base.at[rows], BASE.at[b], ld.at[2]).start()
        dst = pl.ds(pl.multiple_of(b * 256, 256), 256)
        pltpu.make_async_copy(
            tok.at[:, rows], TK.at[pl.ds(c * 128, 128), dst], tk_l
        ).start()
        return 0

    lax.fori_loop(0, 16, load_block, 0)

    wait(CO, ld.at[0])
    wait(SC, ld.at[1])
    own = l * 8 + z
    by_row = SC[...].T
    for g in range(4):
        lanes = pl.ds(g * 128, 128)
        W[own, :, lanes] = (CO[:, lanes].astype(F32) * by_row[:, g : g + 1]).astype(BF16)

    pl.semaphore_wait(barrier, len(peers))

    def half(block, h):
        return W.at[block, pl.ds(h * 128, 128)]

    def send_z(block, t, way, h):
        send(half(block, h), half(block, h), az_s, az_r.at[t, way, h], (up, down)[way])

    def few(block, h):
        return W.at[block, pl.ds(h * 128, 32)]

    def most(block, h):
        return W.at[block, pl.ds(h * 128 + 32, 96)]

    def send_few(block, t, way, h):
        send(few(block, h), few(block, h), bz_s, bz_r.at[t, way, h], (up, down)[way])

    def send_x(block, zz, h):
        send(most(block, h), most(block, h), ax_s, ax_r.at[zz, h], (A, B)[h])

    for d in (1, 3, 2):
        send(cot, CA.at[me8], ca_s, ca_r.at[me8], dev(y=(y + d) % 4))
    send(cot, CA.at[me8], ca_s, ca_r.at[me8], peer)

    def send_tokens(b, _):
        src = pl.ds(col(b, oc), 256)
        dst = pl.ds(pl.multiple_of(b * 256, 256), 256)
        send(tok.at[:, src], TK.at[pl.ds(c * 128, 128), dst], tk_s, tk_r, peer)
        return 0

    my_rows = pl.ds(pl.multiple_of(me8 * 128, 128), 128)

    def kof(i):
        return lax.rem(z // 2 + i + 1, 4)

    def chunk(p, i, j, core):
        return pl.multiple_of(
            ((p * 8 + 2 * kof(i) + j % 2) * 2 + core) * 256 + (j // 2) * 128, 128
        )

    def send_parts(i):
        for e, p in ((0, 1 - l), (1, l)):
            n = 2 * i + e
            dst = TW.at[n, my_rows]
            for d in (1, 3, 2, 0):
                j = (y + d) % 4
                for cc in (c, oc):
                    src = tok.at[:, pl.ds(chunk(p, i, j, cc), 128)]
                    if d == 0 and cc is c:
                        pltpu.make_async_copy(src, dst, tw_r.at[n]).start()
                    else:
                        send(src, dst, tw_s, tw_r.at[n], dev(y=j, c=cc))

    send_parts(0)
    for h in range(2):
        send(half(own, h), half(own, h), ao_s, ax_r.at[z, h], (A, B)[h])
        send_z(own, 0, 0, h)
        send_z(own, 0, 1, h)
    lax.fori_loop(0, 16, send_tokens, 0)
    send_parts(1)

    PA[...] = jnp.zeros_like(PA)
    wait(CA.at[me8], ca_r.at[me8])
    wait(CA.at[y * 2 + oc], ca_r.at[y * 2 + oc])
    wait(BASE, ld.at[2])
    half_tokens = TK.at[pl.ds(0, 128)]
    wait(half_tokens, tk_l)
    wait(half_tokens, tk_r)

    def offset(m):
        return jnp.where(m % 2 == 1, 8 - (m + 1) // 2, m // 2)

    def use_block(other, m):
        zz = lax.rem(z + offset(m), 8)
        block = jnp.where(other, (1 - l) * 8 + zz, l * 8 + zz)

        @pl.when(jnp.logical_and(other, m > 0))
        def _():
            for h in range(2):
                wait(most(block, h), ax_r.at[zz, h])

        w = (BASE[block].astype(F32) + W[block].astype(F32)).astype(BF16)
        lanes = pl.ds(pl.multiple_of(block * 256, 256), 256)
        PA[...] += jnp.dot(TK[:, lanes], w, preferred_element_type=F32)
        both = CA[pl.ds(y * 2, 2)].reshape(256, 512)
        IG[block] = lax.dot_general(
            both, w, (((1,), (1,)), ((), ())), preferred_element_type=F32
        ).astype(BF16)
        out = igrad.at[:, pl.ds(col(block, c), 256)]
        mine = IG.at[block, pl.ds(pl.multiple_of(c * 128, 128), 128)]
        theirs = IG.at[block, pl.ds(pl.multiple_of(oc * 128, 128), 128)]
        send(theirs, out, ig_s, ig_r, peer)
        pltpu.make_async_copy(mine, out, ig_l).start()

    def x_rows(half_x):
        return pl.ds(pl.multiple_of(half_x * 64, 64), 64)

    def x_sum(i):
        wait(XR.at[i], gx_r.at[i])
        total = GF[i % 2, x_rows(X), :]
        for q in range(3):
            total = total + XR[i, q].astype(F32)
        ZS[i] = total.astype(BF16)
        to = 2 * kof(i) + y % 2

        @pl.when(to != z)
        def _():
            send(ZS.at[i], ZR.at[z], zs_s, zs_r, dev(z=to))

        @pl.when(to == z)
        def _():
            ZR[z] = total.astype(BF16)

    def product(n):
        wait(TW.at[n], tw_r.at[n])
        return lax.dot_general(
            TW[n], CA[...].reshape(1024, 512), (((0,), (0,)), ((), ())),
            preferred_element_type=F32,
        )

    def parts(i):
        @pl.when(i == 0)
        def _():
            for d in (1, 3, 2):
                k = ((y + d) % 4) * 2 + c
                wait(CA.at[k], ca_r.at[k])
                send(CA.at[k], CA.at[k], ca_s, ca_r.at[k], peer)
            for d in (1, 3, 2):
                k = ((y + d) % 4) * 2 + oc
                wait(CA.at[k], ca_r.at[k])

        GX[2 * i] = product(2 * i).astype(BF16)
        send(GX.at[2 * i, x_rows(X)], XR.at[i, 0], gx_s, gx_r.at[i], A)
        send(GX.at[2 * i, x_rows(1 - X)], XR.at[i, 1], gx_s, gx_r.at[i], B)
        GF[i % 2] = product(2 * i + 1)
        GX[2 * i + 1] = GF[i % 2].astype(BF16)
        send(GX.at[2 * i + 1, x_rows(1 - X)], XR.at[i, 2], gx_s, gx_r.at[i], O)

    beside = (1 - l) * 8 + z

    def step(i, _):
        @pl.when(i < 4)
        def _():
            t = i

            @pl.when(t == 0)
            def _():
                for h in range(2):
                    wait(half(beside, h), ax_r.at[z, h])
                    send_few(beside, 0, 0, h)
                    send_few(beside, 0, 1, h)

            zu, zd = lax.rem(z + 7 - t, 8), lax.rem(z + t + 1, 8)
            for h in range(2):
                for way, zz in ((0, zu), (1, zd)):
                    block = l * 8 + zz

                    @pl.when(jnp.logical_or(t < 3, h == way))
                    def _():
                        wait(half(block, h), az_r.at[t, way, h])

                        @pl.when(jnp.logical_or(t < 2, jnp.logical_and(t == 2, h == way)))
                        def _():
                            send_z(block, t + 1, way, h)

                        send_x(block, zz, h)

            for h in range(2):
                for way, zz in ((0, zu), (1, zd)):
                    block2 = (1 - l) * 8 + zz

                    @pl.when(jnp.logical_or(t < 3, h == way))
                    def _():
                        wait(few(block2, h), bz_r.at[t, way, h])

                        @pl.when(jnp.logical_or(t < 2, jnp.logical_and(t == 2, h == way)))
                        def _():
                            send_few(block2, t + 1, way, h)

        @pl.when(i < 2)
        def _():
            send_parts(i + 2)

        lo1 = jnp.where(i == 0, 0, jnp.minimum(2 * i + 1, 8))
        hi1 = jnp.minimum(2 * i + 3, 8)
        lo2 = jnp.maximum(2 * i - 1, 0)
        hi2 = jnp.minimum(2 * i + 1, 8)
        n1 = hi1 - lo1

        def one(n, _):
            other = n >= n1
            use_block(other, jnp.where(other, lo2 + n - n1, lo1 + n))
            return 0

        lax.fori_loop(0, n1 + hi2 - lo2, one, 0)

        @pl.when(i == 4)
        def _():
            send(PA.at[pl.ds(pl.multiple_of(oc * 128, 128), 128)], PR, pa_s, pa_r, peer)

        @pl.when(i > 0)
        def _():
            x_sum(i - 1)

        @pl.when(i < 4)
        def _():
            parts(i)

        return 0

    lax.fori_loop(0, 5, step, 0)

    holds = z % 2 == y % 2
    slot = (y // 2) * 2 + X

    @pl.when(holds)
    def _():
        wait(ZR.at[pl.ds(0, 7)], zs_r)
        total = ZR[0].astype(F32)
        for q in range(1, 8):
            total = total + ZR[q].astype(F32)
        total = (total * (1.0 / math.sqrt(32768.0))).astype(BF16)
        RB[...] = total
        for XX in (X, 1 - X):
            for d in (1, 2, 3, 0):
                if XX is X and d == 0:
                    continue
                send(RB, RR.at[slot], rr_s, rr_r, dev(X=XX, y=(y + d) % 4))
        RR[slot] = total

    wait(PR, pa_r)
    proj[...] = (PA[pl.ds(pl.multiple_of(c * 128, 128), 128), :] + PR[...]).astype(BF16)

    @pl.when(holds)
    def _():
        wait(RR.at[pl.ds(0, 3)], rr_r)

    @pl.when(jnp.logical_not(holds))
    def _():
        wait(RR, rr_r)

    for q in range(4):
        wgrad[pl.ds(q * 64, 64), :] = RR[q].astype(F32)

    wait(half_tokens, tk_s)
    wait(CA.at[pl.ds(0, 7)], ca_s)
    wait(TW.at[:, pl.ds(0, 896)], tw_s)
    wait(W.at[pl.ds(0, 7)], az_s)
    wait(W.at[pl.ds(0, 7), pl.ds(0, 64)], bz_s)
    wait(W.at[0], ao_s)
    wait(W.at[pl.ds(0, 7), pl.ds(0, 192)], ax_s)
    wait(XR, gx_s)
    wait(PR, pa_s)

    @pl.when(holds)
    def _():
        wait(ZS.at[pl.ds(0, 3)], zs_s)
        wait(ZR.at[pl.ds(0, 7)], rr_s)

    @pl.when(jnp.logical_not(holds))
    def _():
        wait(ZS, zs_s)

    wait(half_tokens, ig_s)
    wait(half_tokens, ig_l)
    wait(half_tokens, ig_r)


def finish(p_in, i_in, w_in, p_out, i_out, w_out, p_buf, i_buf, w_buf, sem_in, sem_out):
    pieces = [(w_in, w_buf, w_out)]
    pieces += [
        tuple(ref.at[pl.ds(n * 32, 32)] for ref in (i_in, i_buf, i_out)) for n in range(4)
    ]
    pieces += [(p_in, p_buf, p_out)]
    loads = [
        pltpu.make_async_copy(src, buf, sem_in.at[n]) for n, (src, buf, _) in enumerate(pieces)
    ]
    stores = [
        pltpu.make_async_copy(buf, dst, sem_out.at[n]) for n, (_, buf, dst) in enumerate(pieces)
    ]
    for load in loads:
        load.start()
    for load, store in zip(loads, stores):
        load.wait()
        store.start()
    for store in stores:
        store.wait()


def body(tokens, cotangent, base_copy, codes, scales):
    dma = pltpu.SemaphoreType.DMA
    anywhere = pl.BlockSpec(memory_space=pl.ANY)
    shapes = (
        jax.ShapeDtypeStruct((128, 512), BF16),
        jax.ShapeDtypeStruct((128, 8192), BF16),
        jax.ShapeDtypeStruct((256, 512), F32),
    )
    results = pl.pallas_call(
        kernel,
        out_shape=shapes,
        in_specs=[anywhere] * 5,
        out_specs=(
            pl.BlockSpec(memory_space=pltpu.VMEM),
            anywhere,
            pl.BlockSpec(memory_space=pltpu.VMEM),
        ),
        scratch_shapes=[
            pltpu.VMEM((16, 256, 512), BF16),
            pltpu.VMEM((16, 256, 512), BF16),
            pltpu.VMEM((256, 4096), BF16),
            pltpu.VMEM((8, 128, 512), BF16),
            pltpu.VMEM((8, 1024, 128), BF16),
            pltpu.VMEM((2, 128, 512), F32),
            pltpu.VMEM((8, 128, 512), BF16),
            pltpu.VMEM((4, 3, 64, 512), BF16),
            pltpu.VMEM((4, 64, 512), BF16),
            pltpu.VMEM((8, 64, 512), BF16),
            pltpu.VMEM((64, 512), BF16),
            pltpu.VMEM((4, 64, 512), BF16),
            pltpu.VMEM((16, 256, 256), BF16),
            pltpu.VMEM((256, 512), F32),
            pltpu.VMEM((128, 512), F32),
            pltpu.VMEM((256, 512), jnp.int32),
            pltpu.VMEM((4, 256), F32),
            dma((3,)),
            dma, dma, dma,
            dma, dma((8,)),
            dma, dma((8,)),
            dma, dma((4, 2, 2)),
            dma, dma((4, 2, 2)),
            dma,
            dma, dma((8, 2)),
            dma, dma, dma,
            dma, dma((4,)),
            dma, dma,
            dma, dma,
            dma, dma,
        ],
        compiler_params=pltpu.CompilerParams(
            collective_id=0, has_side_effects=True, vmem_limit_bytes=62 << 20
        ),
        cost_estimate=pl.CostEstimate(
            flops=6 * 128 * 8192 * 512, bytes_accessed=24 << 20, transcendentals=0
        ),
    )(tokens, cotangent, base_copy, codes, scales.T)
    return pl.pallas_call(
        finish,
        out_shape=shapes,
        in_specs=[anywhere] * 3,
        out_specs=(anywhere,) * 3,
        scratch_shapes=[
            pltpu.VMEM((128, 512), BF16),
            pltpu.VMEM((128, 8192), BF16),
            pltpu.VMEM((256, 512), F32),
            dma((6,)),
            dma((6,)),
        ],
        compiler_params=pltpu.CompilerParams(vmem_limit_bytes=62 << 20),
    )(*results)


def solution(mesh):
    return jax.shard_map(
        body,
        mesh=mesh,
        in_specs=(
            P(("replica", "shard"), None),
            P(("replica", "shard"), None),
            P(),
            P("shard", None),
            P("shard", None),
        ),
        out_specs=(P(("replica", "shard"), None), P(("replica", "shard"), None), P("shard", None)),
        check_vma=False,
    )
```

```python
import math

import jax
import jax.numpy as jnp
from jax import lax
from jax.experimental import pallas as pl
from jax.experimental.pallas import tpu as pltpu
from jax.sharding import PartitionSpec as P

BF16 = jnp.bfloat16
F32 = jnp.float32


def kernel(
    tok, cot, base, codes, scales,
    proj, igrad, wgrad,
    W, BASE, TOK, TT, TK, CA, TW, GF, GX, XR, ZS, ZR, RR, IG, PA, PR, CO, SC,
    ld, tk_l, tk_s, tk_r, ca_s, ca_r, tw_s, tw_r, az_s, az_r, bz_s, bz_r, ao_s, ax_s, ax_r,
    ig_l, ig_s, ig_r, gx_s, gx_r, zs_s, zs_r, rr_s, rr_r, pa_s, pa_r,
):
    r = lax.axis_index("replica")
    s = lax.axis_index("shard")
    X, y = r // 4, r % 4
    l, z, c = s // 16, (s % 16) // 2, s % 2
    oc = 1 - c

    def dev(X=X, y=y, l=l, z=z, c=c):
        return {"replica": X * 4 + y, "shard": l * 16 + z * 2 + c}

    up, down = dev(z=(z + 1) % 8), dev(z=(z + 7) % 8)
    A, B, O = dev(l=1 - l), dev(X=1 - X, l=1 - l), dev(X=1 - X)
    peer = dev(c=oc)

    def wait(ref, sem):
        pltpu.make_async_copy(ref, ref, sem).wait()

    def send(src, dst, ssem, rsem, to):
        pltpu.make_async_remote_copy(src, dst, ssem, rsem, device_id=to).start()

    pltpu.make_async_copy(tok, TOK, ld.at[3]).start()
    pltpu.make_async_copy(codes, CO, ld.at[0]).start()
    pltpu.make_async_copy(scales, SC, ld.at[1]).start()
    me8 = y * 2 + c
    pltpu.make_async_copy(cot, CA.at[me8], ca_r.at[me8]).start()

    barrier = pltpu.get_barrier_semaphore()
    peers = [peer]
    peers += [dev(y=(y + d) % 4, c=cc) for d in (1, 2, 3) for cc in (c, oc)]
    peers += [dev(z=(z + d) % 8) for d in range(1, 8)]
    peers += [A, B, O]
    peers += [dev(X=1 - X, y=(y + d) % 4) for d in (1, 2, 3)]
    for d in peers:
        pl.semaphore_signal(barrier, 1, device_id=d)

    def col(block, core):
        return pl.multiple_of((block * 2 + core) * 256, 256)

    def load_block(b, _):
        rows = pl.ds(col(b, c), 256)
        pltpu.make_async_copy(base.at[rows], BASE.at[b], ld.at[2]).start()
        dst = pl.ds(pl.multiple_of(b * 256, 256), 256)
        pltpu.make_async_copy(
            tok.at[:, rows], TK.at[pl.ds(c * 128, 128), dst], tk_l
        ).start()
        return 0

    lax.fori_loop(0, 16, load_block, 0)

    wait(CO, ld.at[0])
    wait(SC, ld.at[1])
    own = l * 8 + z
    by_row = SC[...].T
    for g in range(4):
        lanes = pl.ds(g * 128, 128)
        W[own, :, lanes] = (CO[:, lanes].astype(F32) * by_row[:, g : g + 1]).astype(BF16)

    def zof(n):
        return lax.rem(z + jnp.where(n % 2 == 1, (7 - n) // 2, 4 + n // 2), 8)

    def turn(n):
        def one(q, _):
            p, cc = q // 2, q % 2
            lanes = pl.ds(col(p * 8 + zof(n), cc), 256)
            TT[n, cc, p] = TOK[:, lanes].T
            return 0

        lax.fori_loop(0, 4, one, 0)

    wait(TOK, ld.at[3])
    turn(0)
    turn(1)

    pl.semaphore_wait(barrier, len(peers))

    def half(block, h):
        return W.at[block, pl.ds(h * 128, 128)]

    def send_z(block, t, way, h):
        send(half(block, h), half(block, h), az_s, az_r.at[t, way, h], (up, down)[way])

    def few(block, h):
        return W.at[block, pl.ds(h * 128, 32)]

    def most(block, h):
        return W.at[block, pl.ds(h * 128 + 32, 96)]

    def send_few(block, t, way, h):
        send(few(block, h), few(block, h), bz_s, bz_r.at[t, way, h], (up, down)[way])

    def send_x(block, zz, h):
        send(most(block, h), most(block, h), ax_s, ax_r.at[zz, h], (A, B)[h])

    for d in (1, 3, 2):
        send(cot, CA.at[me8], ca_s, ca_r.at[me8], dev(y=(y + d) % 4))
    send(cot, CA.at[me8], ca_s, ca_r.at[me8], peer)

    def send_tokens(b, _):
        src = pl.ds(col(b, oc), 256)
        dst = pl.ds(pl.multiple_of(b * 256, 256), 256)
        send(tok.at[:, src], TK.at[pl.ds(c * 128, 128), dst], tk_s, tk_r, peer)
        return 0

    my_lanes = pl.ds(pl.multiple_of(me8 * 128, 128), 128)

    def send_part(n):
        dst = TW.at[n, :, :, my_lanes]
        for d in (1, 3, 2, 0):
            j = (y + d) % 4
            rows = pl.ds(pl.multiple_of(j * 64, 64), 64)
            for cc in (c, oc):
                src = TT.at[n, cc, :, rows]
                if d == 0 and cc is c:
                    pltpu.make_async_copy(src, dst, tw_r.at[n]).start()
                else:
                    send(src, dst, tw_s, tw_r.at[n], dev(y=j, c=cc))

    send_part(0)
    for h in range(2):
        send(half(own, h), half(own, h), ao_s, ax_r.at[z, h], (A, B)[h])
        send_z(own, 0, 0, h)
        send_z(own, 0, 1, h)
    lax.fori_loop(0, 16, send_tokens, 0)
    send_part(1)
    for n in (2, 3):
        turn(n)
        send_part(n)

    PA[...] = jnp.zeros_like(PA)
    wait(CA.at[me8], ca_r.at[me8])
    wait(CA.at[y * 2 + oc], ca_r.at[y * 2 + oc])
    wait(BASE, ld.at[2])
    half_tokens = TK.at[pl.ds(0, 128)]
    wait(half_tokens, tk_l)
    wait(half_tokens, tk_r)

    def offset(m):
        return jnp.where(m % 2 == 1, 8 - (m + 1) // 2, m // 2)

    def use_block(other, m):
        zz = lax.rem(z + offset(m), 8)
        block = jnp.where(other, (1 - l) * 8 + zz, l * 8 + zz)

        @pl.when(jnp.logical_and(other, m > 0))
        def _():
            for h in range(2):
                wait(most(block, h), ax_r.at[zz, h])

        w = (BASE[block].astype(F32) + W[block].astype(F32)).astype(BF16)
        lanes = pl.ds(pl.multiple_of(block * 256, 256), 256)
        PA[...] += jnp.dot(TK[:, lanes], w, preferred_element_type=F32)
        both = CA[pl.ds(y * 2, 2)].reshape(256, 512)
        IG[block] = lax.dot_general(
            both, w, (((1,), (1,)), ((), ())), preferred_element_type=F32
        ).astype(BF16)
        out = igrad.at[:, pl.ds(col(block, c), 256)]
        mine = IG.at[block, pl.ds(pl.multiple_of(c * 128, 128), 128)]
        theirs = IG.at[block, pl.ds(pl.multiple_of(oc * 128, 128), 128)]
        send(theirs, out, ig_s, ig_r, peer)
        pltpu.make_async_copy(mine, out, ig_l).start()

    def x_rows(p, half_x):
        return pl.ds(pl.multiple_of(p * 64 + half_x * 32, 32), 32)

    def part(n):
        @pl.when(n == 0)
        def _():
            for d in (1, 3, 2):
                k = ((y + d) % 4) * 2 + c
                wait(CA.at[k], ca_r.at[k])
                send(CA.at[k], CA.at[k], ca_s, ca_r.at[k], peer)
            for d in (1, 3, 2):
                k = ((y + d) % 4) * 2 + oc
                wait(CA.at[k], ca_r.at[k])

        wait(TW.at[n], tw_r.at[n])
        GF[n % 4] = jnp.dot(
            TW[n].reshape(128, 1024), CA[...].reshape(1024, 512), preferred_element_type=F32
        )
        GX[n] = GF[n % 4].astype(BF16)
        send(GX.at[n, x_rows(l, 1 - X)], XR.at[n, 2], gx_s, gx_r.at[n], O)
        send(GX.at[n, x_rows(1 - l, X)], XR.at[n, 0], gx_s, gx_r.at[n], A)
        send(GX.at[n, x_rows(1 - l, 1 - X)], XR.at[n, 1], gx_s, gx_r.at[n], B)

    def x_sum(n):
        wait(XR.at[n], gx_r.at[n])
        total = GF[n % 4, x_rows(l, X), :]
        for q in range(3):
            total = total + XR[n, q].astype(F32)
        return total

    def x_stage(n):
        ZS[n] = x_sum(n).astype(BF16)
        send(ZS.at[n], ZR.at[z], zs_s, zs_r, dev(z=zof(n)))

    beside = (1 - l) * 8 + z

    def step(i, _):
        t = i

        @pl.when(t == 0)
        def _():
            for h in range(2):
                wait(half(beside, h), ax_r.at[z, h])
                send_few(beside, 0, 0, h)
                send_few(beside, 0, 1, h)

        zu, zd = lax.rem(z + 7 - t, 8), lax.rem(z + t + 1, 8)
        for h in range(2):
            for way, zz in ((0, zu), (1, zd)):
                block = l * 8 + zz

                @pl.when(jnp.logical_or(t < 3, h == way))
                def _():
                    wait(half(block, h), az_r.at[t, way, h])

                    @pl.when(jnp.logical_or(t < 2, jnp.logical_and(t == 2, h == way)))
                    def _():
                        send_z(block, t + 1, way, h)

                    send_x(block, zz, h)

        for h in range(2):
            for way, zz in ((0, zu), (1, zd)):
                block2 = (1 - l) * 8 + zz

                @pl.when(jnp.logical_or(t < 3, h == way))
                def _():
                    wait(few(block2, h), bz_r.at[t, way, h])

                    @pl.when(jnp.logical_or(t < 2, jnp.logical_and(t == 2, h == way)))
                    def _():
                        send_few(block2, t + 1, way, h)

        @pl.when(i < 2)
        def _():
            for e in range(2):
                turn(2 * i + 4 + e)
                send_part(2 * i + 4 + e)

        lo1 = jnp.where(i == 0, 0, 2 * i + 1)
        n1 = jnp.minimum(2 * i + 3, 8) - lo1
        lo2 = jnp.maximum(2 * i - 3, 0)
        n2 = jnp.maximum(2 * i - 1, 0) - lo2

        def one(n, _):
            other = n >= n1
            use_block(other, jnp.where(other, lo2 + n - n1, lo1 + n))
            return 0

        lax.fori_loop(0, n1 + n2, one, 0)

        for n in (2 * i, 2 * i + 1):

            @pl.when(i > 0)
            def _():
                x_stage(n - 2)

            part(n)

        return 0

    lax.fori_loop(0, 4, step, 0)

    x_stage(6)
    total = x_sum(7)
    wait(ZR.at[pl.ds(0, 7)], zs_r)
    for d in range(1, 8):
        total = total + ZR[lax.rem(z + d, 8)].astype(F32)
    my_piece = pl.ds(pl.multiple_of((y * 2 + X) * 32, 32), 32)
    RR[my_piece, :] = (total * (1.0 / math.sqrt(32768.0))).astype(BF16)
    for XX in (1 - X, X):
        for d in (2, 1, 3, 0):
            if XX is X and d == 0:
                continue
            to = dev(X=XX, y=(y + d) % 4)
            send(RR.at[my_piece], RR.at[my_piece], rr_s, rr_r, to)

    def last(m, _):
        use_block(True, m)
        return 0

    lax.fori_loop(5, 8, last, 0)
    send(PA.at[pl.ds(pl.multiple_of(oc * 128, 128), 128)], PR, pa_s, pa_r, peer)

    wait(PR, pa_r)
    proj[...] = (PA[pl.ds(pl.multiple_of(c * 128, 128), 128), :] + PR[...]).astype(BF16)

    wait(RR.at[pl.ds(0, 224)], rr_r)
    wgrad[...] = RR[...].astype(F32)

    wait(half_tokens, tk_s)
    wait(CA.at[pl.ds(0, 7)], ca_s)
    wait(TW.at[:, :, :, pl.ds(0, 896)], tw_s)
    wait(W.at[pl.ds(0, 7)], az_s)
    wait(W.at[pl.ds(0, 7), pl.ds(0, 64)], bz_s)
    wait(W.at[0], ao_s)
    wait(W.at[pl.ds(0, 7), pl.ds(0, 192)], ax_s)
    wait(XR, gx_s)
    wait(PR, pa_s)

    wait(ZS, zs_s)
    wait(ZR.at[pl.ds(0, 7)], rr_s)
    wait(half_tokens, ig_s)
    wait(half_tokens, ig_l)
    wait(half_tokens, ig_r)


def finish(p_in, i_in, w_in, p_out, i_out, w_out, p_buf, i_buf, w_buf, sem_in, sem_out):
    pieces = [(w_in, w_buf, w_out)]
    pieces += [
        tuple(ref.at[pl.ds(n * 32, 32)] for ref in (i_in, i_buf, i_out)) for n in range(4)
    ]
    pieces += [(p_in, p_buf, p_out)]
    loads = [
        pltpu.make_async_copy(src, buf, sem_in.at[n]) for n, (src, buf, _) in enumerate(pieces)
    ]
    stores = [
        pltpu.make_async_copy(buf, dst, sem_out.at[n]) for n, (_, buf, dst) in enumerate(pieces)
    ]
    for load in loads:
        load.start()
    for load, store in zip(loads, stores):
        load.wait()
        store.start()
    for store in stores:
        store.wait()


def body(tokens, cotangent, base_copy, codes, scales):
    dma = pltpu.SemaphoreType.DMA
    anywhere = pl.BlockSpec(memory_space=pl.ANY)
    shapes = (
        jax.ShapeDtypeStruct((128, 512), BF16),
        jax.ShapeDtypeStruct((128, 8192), BF16),
        jax.ShapeDtypeStruct((256, 512), F32),
    )
    results = pl.pallas_call(
        kernel,
        out_shape=shapes,
        in_specs=[anywhere] * 5,
        out_specs=(
            pl.BlockSpec(memory_space=pltpu.VMEM),
            anywhere,
            pl.BlockSpec(memory_space=pltpu.VMEM),
        ),
        scratch_shapes=[
            pltpu.VMEM((16, 256, 512), BF16),
            pltpu.VMEM((16, 256, 512), BF16),
            pltpu.VMEM((128, 8192), BF16),
            pltpu.VMEM((8, 2, 2, 256, 128), BF16),
            pltpu.VMEM((256, 4096), BF16),
            pltpu.VMEM((8, 128, 512), BF16),
            pltpu.VMEM((8, 2, 64, 1024), BF16),
            pltpu.VMEM((4, 128, 512), F32),
            pltpu.VMEM((8, 128, 512), BF16),
            pltpu.VMEM((8, 3, 32, 512), BF16),
            pltpu.VMEM((7, 32, 512), BF16),
            pltpu.VMEM((8, 32, 512), BF16),
            pltpu.VMEM((256, 512), BF16),
            pltpu.VMEM((16, 256, 256), BF16),
            pltpu.VMEM((256, 512), F32),
            pltpu.VMEM((128, 512), F32),
            pltpu.VMEM((256, 512), jnp.int32),
            pltpu.VMEM((4, 256), F32),
            dma((4,)),
            dma, dma, dma,
            dma, dma((8,)),
            dma, dma((8,)),
            dma, dma((4, 2, 2)),
            dma, dma((4, 2, 2)),
            dma,
            dma, dma((8, 2)),
            dma, dma, dma,
            dma, dma((8,)),
            dma, dma,
            dma, dma,
            dma, dma,
        ],
        compiler_params=pltpu.CompilerParams(
            collective_id=0, has_side_effects=True, vmem_limit_bytes=62 << 20
        ),
        cost_estimate=pl.CostEstimate(
            flops=6 * 128 * 8192 * 512, bytes_accessed=24 << 20, transcendentals=0
        ),
    )(tokens, cotangent, base_copy, codes, scales.T)
    return pl.pallas_call(
        finish,
        out_shape=shapes,
        in_specs=[anywhere] * 3,
        out_specs=(anywhere,) * 3,
        scratch_shapes=[
            pltpu.VMEM((128, 512), BF16),
            pltpu.VMEM((128, 8192), BF16),
            pltpu.VMEM((256, 512), F32),
            dma((6,)),
            dma((6,)),
        ],
        compiler_params=pltpu.CompilerParams(vmem_limit_bytes=62 << 20),
    )(*results)


def solution(mesh):
    return jax.shard_map(
        body,
        mesh=mesh,
        in_specs=(
            P(("replica", "shard"), None),
            P(("replica", "shard"), None),
            P(),
            P("shard", None),
            P("shard", None),
        ),
        out_specs=(P(("replica", "shard"), None), P(("replica", "shard"), None), P("shard", None)),
        check_vma=False,
    )
```

```python
import math

import jax
import jax.numpy as jnp
from jax import lax
from jax.experimental import pallas as pl
from jax.experimental.pallas import tpu as pltpu
from jax.sharding import PartitionSpec as P

BF16 = jnp.bfloat16
F32 = jnp.float32


def kernel(
    tok, cot, base, codes, scales,
    proj, igrad, wgrad,
    W, BASE, TOK, TT, TK, CA, TW, GF, GX, XR, ZS, ZR, RR, IG, PA, PR, CO, SC,
    ld, tk_l, tk_s, tk_r, ca_s, ca_r, tw_s, tw_r, az_s, az_r, bz_s, bz_r, ao_s, ax_s, ax_r,
    ig_l, ig_s, ig_r, gx_s, gx_r, zs_s, zs_r, rr_s, rr_r, pa_s, pa_r,
):
    r = lax.axis_index("replica")
    s = lax.axis_index("shard")
    X, y = r // 4, r % 4
    l, z, c = s // 16, (s % 16) // 2, s % 2
    oc = 1 - c

    def dev(X=X, y=y, l=l, z=z, c=c):
        return {"replica": X * 4 + y, "shard": l * 16 + z * 2 + c}

    up, down = dev(z=(z + 1) % 8), dev(z=(z + 7) % 8)
    A, B, O = dev(l=1 - l), dev(X=1 - X, l=1 - l), dev(X=1 - X)
    peer = dev(c=oc)

    def wait(ref, sem):
        pltpu.make_async_copy(ref, ref, sem).wait()

    def send(src, dst, ssem, rsem, to):
        pltpu.make_async_remote_copy(src, dst, ssem, rsem, device_id=to).start()

    pltpu.make_async_copy(tok, TOK, ld.at[3]).start()
    pltpu.make_async_copy(codes, CO, ld.at[0]).start()
    pltpu.make_async_copy(scales, SC, ld.at[1]).start()
    me8 = y * 2 + c
    pltpu.make_async_copy(cot, CA.at[me8], ca_r.at[me8]).start()

    barrier = pltpu.get_barrier_semaphore()
    peers = [peer]
    peers += [dev(y=(y + d) % 4, c=cc) for d in (1, 2, 3) for cc in (c, oc)]
    peers += [up, down]
    peers += [A, B, O]
    peers += [dev(X=1 - X, y=(y + d) % 4) for d in (1, 2, 3)]
    for d in peers:
        pl.semaphore_signal(barrier, 1, device_id=d)

    def col(block, core):
        return pl.multiple_of((block * 2 + core) * 256, 256)

    def load_block(b, _):
        rows = pl.ds(col(b, c), 256)
        pltpu.make_async_copy(base.at[rows], BASE.at[b], ld.at[2]).start()
        dst = pl.ds(pl.multiple_of(b * 256, 256), 256)
        pltpu.make_async_copy(
            tok.at[:, rows], TK.at[pl.ds(c * 128, 128), dst], tk_l
        ).start()
        return 0

    lax.fori_loop(0, 16, load_block, 0)

    def zof(n):
        return lax.rem(z + jnp.where(n % 2 == 1, 8 - (7 - n) // 2, 4 - n // 2), 8)

    def turn(n):
        def one(q, _):
            p, cc = q // 2, q % 2
            lanes = pl.ds(col(p * 8 + zof(n), cc), 256)
            TT[n, cc, p] = TOK[:, lanes].T
            return 0

        lax.fori_loop(0, 4, one, 0)

    pl.semaphore_wait(barrier, len(peers))

    def half(block, h):
        return W.at[block, pl.ds(h * 128, 128)]

    def send_z(block, t, way, h):
        send(half(block, h), half(block, h), az_s, az_r.at[t, way, h], (up, down)[way])

    def few(block, h):
        return W.at[block, pl.ds(h * 128, 48)]

    def most(block, h):
        return W.at[block, pl.ds(h * 128 + 48, 80)]

    def send_few(block, t, way, h):
        send(few(block, h), few(block, h), bz_s, bz_r.at[t, way, h], (up, down)[way])

    def send_x(block, zz, h):
        send(most(block, h), most(block, h), ax_s, ax_r.at[zz, h], (A, B)[h])

    for d in (1, 3, 2):
        send(cot, CA.at[me8], ca_s, ca_r.at[me8], dev(y=(y + d) % 4))
    send(cot, CA.at[me8], ca_s, ca_r.at[me8], peer)

    def send_tokens(b, _):
        src = pl.ds(col(b, oc), 256)
        dst = pl.ds(pl.multiple_of(b * 256, 256), 256)
        send(tok.at[:, src], TK.at[pl.ds(c * 128, 128), dst], tk_s, tk_r, peer)
        return 0

    my_lanes = pl.ds(pl.multiple_of(me8 * 128, 128), 128)

    def send_part(n):
        dst = TW.at[n, :, :, my_lanes]
        for d in (1, 3, 2, 0):
            j = (y + d) % 4
            rows = pl.ds(pl.multiple_of(j * 64, 64), 64)
            for cc in (c, oc):
                src = TT.at[n, cc, :, rows]
                if d == 0 and cc is c:
                    pltpu.make_async_copy(src, dst, tw_r.at[n]).start()
                else:
                    send(src, dst, tw_s, tw_r.at[n], dev(y=j, c=cc))

    wait(CO, ld.at[0])
    wait(SC, ld.at[1])
    own = l * 8 + z
    by_row = SC[...].T
    for g in range(4):
        lanes = pl.ds(g * 128, 128)
        W[own, :, lanes] = (CO[:, lanes].astype(F32) * by_row[:, g : g + 1]).astype(BF16)
    for h in range(2):
        send(half(own, h), half(own, h), ao_s, ax_r.at[z, h], (A, B)[h])
        send_z(own, 0, 0, h)
        send_z(own, 0, 1, h)
    wait(TOK, ld.at[3])
    for n in range(4):
        turn(n)
        send_part(n)
    lax.fori_loop(0, 16, send_tokens, 0)

    PA[...] = jnp.zeros_like(PA)
    wait(CA.at[me8], ca_r.at[me8])
    wait(CA.at[y * 2 + oc], ca_r.at[y * 2 + oc])
    wait(BASE, ld.at[2])
    half_tokens = TK.at[pl.ds(0, 128)]
    wait(half_tokens, tk_l)
    wait(half_tokens, tk_r)

    def offset(m):
        return jnp.where(m % 2 == 1, 8 - (m + 1) // 2, m // 2)

    def use_block(other, m):
        zz = lax.rem(z + offset(m), 8)
        block = jnp.where(other, 1 - l, l) * 8 + zz

        def arrive():
            for h in range(2):
                wait(most(block, h), ax_r.at[zz, h])

        if other is True:
            arrive()
        else:
            pl.when(jnp.logical_and(other, m > 0))(arrive)

        w = (BASE[block].astype(F32) + W[block].astype(F32)).astype(BF16)
        lanes = pl.ds(pl.multiple_of(block * 256, 256), 256)
        PA[...] += jnp.dot(TK[:, lanes], w, preferred_element_type=F32)
        both = CA[pl.ds(y * 2, 2)].reshape(256, 512)
        IG[block] = lax.dot_general(
            both, w, (((1,), (1,)), ((), ())), preferred_element_type=F32
        ).astype(BF16)
        out = igrad.at[:, pl.ds(col(block, c), 256)]
        mine = IG.at[block, pl.ds(pl.multiple_of(c * 128, 128), 128)]
        theirs = IG.at[block, pl.ds(pl.multiple_of(oc * 128, 128), 128)]
        send(theirs, out, ig_s, ig_r, peer)
        pltpu.make_async_copy(mine, out, ig_l).start()

    def x_rows(p, half_x):
        return pl.ds(pl.multiple_of(p * 64 + half_x * 32, 32), 32)

    def part(n):
        @pl.when(n == 0)
        def _():
            for d in (1, 3, 2):
                k = ((y + d) % 4) * 2 + c
                wait(CA.at[k], ca_r.at[k])
                send(CA.at[k], CA.at[k], ca_s, ca_r.at[k], peer)
            for d in (1, 3, 2):
                k = ((y + d) % 4) * 2 + oc
                wait(CA.at[k], ca_r.at[k])

        wait(TW.at[n], tw_r.at[n])
        GF[n % 4] = jnp.dot(
            TW[n].reshape(128, 1024), CA[...].reshape(1024, 512), preferred_element_type=F32
        )
        GX[n] = GF[n % 4].astype(BF16)
        send(GX.at[n, x_rows(l, 1 - X)], XR.at[n, 2], gx_s, gx_r.at[n], O)
        send(GX.at[n, x_rows(1 - l, X)], XR.at[n, 0], gx_s, gx_r.at[n], A)
        send(GX.at[n, x_rows(1 - l, 1 - X)], XR.at[n, 1], gx_s, gx_r.at[n], B)

    def x_sum(n):
        wait(XR.at[n], gx_r.at[n])
        total = GF[n % 4, x_rows(l, X), :]
        for q in range(3):
            total = total + XR[n, q].astype(F32)
        return total

    def x_stage(n, even):
        total = x_sum(n)

        def pass_on():
            wait(ZR.at[n - 2], zs_r.at[n - 2])
            ZS[n] = (total + ZR[n - 2].astype(F32)).astype(BF16)

        if isinstance(n, int):
            pass_on()
        else:
            pl.when(n >= 2)(pass_on)

            @pl.when(n < 2)
            def _():
                ZS[n] = total.astype(BF16)

        send(ZS.at[n], ZR.at[n], zs_s, zs_r.at[n], up if even else down)

    beside = (1 - l) * 8 + z

    def step(i, _):
        t = i

        @pl.when(t == 0)
        def _():
            for h in range(2):
                wait(half(beside, h), ax_r.at[z, h])
                send_few(beside, 0, 0, h)
                send_few(beside, 0, 1, h)

        zu, zd = lax.rem(z + 7 - t, 8), lax.rem(z + t + 1, 8)
        for h in range(2):
            for way, zz in ((0, zu), (1, zd)):
                block = l * 8 + zz

                @pl.when(jnp.logical_or(t < 3, h == way))
                def _():
                    wait(half(block, h), az_r.at[t, way, h])

                    @pl.when(jnp.logical_or(t < 2, jnp.logical_and(t == 2, h == way)))
                    def _():
                        send_z(block, t + 1, way, h)

                    send_x(block, zz, h)

        for h in range(2):
            for way, zz in ((0, zu), (1, zd)):
                block2 = (1 - l) * 8 + zz

                @pl.when(jnp.logical_or(t < 3, h == way))
                def _():
                    wait(few(block2, h), bz_r.at[t, way, h])

                    @pl.when(jnp.logical_or(t < 2, jnp.logical_and(t == 2, h == way)))
                    def _():
                        send_few(block2, t + 1, way, h)

        @pl.when(i < 2)
        def _():
            for e in range(2):
                turn(2 * i + 4 + e)
                send_part(2 * i + 4 + e)

        lo1 = jnp.where(i == 0, 0, 2 * i + 1)
        n1 = jnp.minimum(2 * i + 3, 8) - lo1
        lo2 = jnp.maximum(2 * i - 3, 0)
        n2 = jnp.maximum(2 * i - 1, 0) - lo2

        def one(n, _):
            other = n >= n1
            use_block(other, jnp.where(other, lo2 + n - n1, lo1 + n))
            return 0

        lax.fori_loop(0, n1 + n2, one, 0)

        for e in range(2):
            n = 2 * i + e

            @pl.when(i > 0)
            def _():
                x_stage(n - 2, e == 0)

            part(n)

        return 0

    lax.fori_loop(0, 4, step, 0)

    use_block(True, 5)
    x_stage(6, True)
    use_block(True, 6)
    total = x_sum(7)
    for n in (5, 6):
        wait(ZR.at[n], zs_r.at[n])
        total = total + ZR[n].astype(F32)
    my_piece = pl.ds(pl.multiple_of((y * 2 + X) * 32, 32), 32)
    RR[my_piece, :] = (total * (1.0 / math.sqrt(32768.0))).astype(BF16)
    for XX in (1 - X, X):
        for d in (2, 1, 3, 0):
            if XX is X and d == 0:
                continue
            to = dev(X=XX, y=(y + d) % 4)
            send(RR.at[my_piece], RR.at[my_piece], rr_s, rr_r, to)

    use_block(True, 7)
    send(PA.at[pl.ds(pl.multiple_of(oc * 128, 128), 128)], PR, pa_s, pa_r, peer)

    wait(PR, pa_r)
    proj[...] = (PA[pl.ds(pl.multiple_of(c * 128, 128), 128), :] + PR[...]).astype(BF16)

    wait(RR.at[pl.ds(0, 224)], rr_r)
    wgrad[...] = RR[...].astype(F32)

    wait(half_tokens, tk_s)
    wait(CA.at[pl.ds(0, 7)], ca_s)
    wait(TW.at[:, :, :, pl.ds(0, 896)], tw_s)
    wait(W.at[pl.ds(0, 7)], az_s)
    wait(W.at[pl.ds(0, 7), pl.ds(0, 96)], bz_s)
    wait(W.at[0], ao_s)
    wait(W.at[pl.ds(0, 7), pl.ds(0, 160)], ax_s)
    wait(XR, gx_s)
    wait(PR, pa_s)

    wait(ZS, zs_s)
    wait(ZR, rr_s)
    wait(half_tokens, ig_s)
    wait(half_tokens, ig_l)
    wait(half_tokens, ig_r)


def finish(p_in, i_in, w_in, p_out, i_out, w_out, p_buf, i_buf, w_buf, sem_in, sem_out):
    pieces = [(w_in, w_buf, w_out)]
    pieces += [
        tuple(ref.at[pl.ds(n * 32, 32)] for ref in (i_in, i_buf, i_out)) for n in range(4)
    ]
    pieces += [(p_in, p_buf, p_out)]
    loads = [
        pltpu.make_async_copy(src, buf, sem_in.at[n]) for n, (src, buf, _) in enumerate(pieces)
    ]
    stores = [
        pltpu.make_async_copy(buf, dst, sem_out.at[n]) for n, (_, buf, dst) in enumerate(pieces)
    ]
    for load in loads:
        load.start()
    for load, store in zip(loads, stores):
        load.wait()
        store.start()
    for store in stores:
        store.wait()


def body(tokens, cotangent, base_copy, codes, scales):
    dma = pltpu.SemaphoreType.DMA
    anywhere = pl.BlockSpec(memory_space=pl.ANY)
    shapes = (
        jax.ShapeDtypeStruct((128, 512), BF16),
        jax.ShapeDtypeStruct((128, 8192), BF16),
        jax.ShapeDtypeStruct((256, 512), F32),
    )
    results = pl.pallas_call(
        kernel,
        out_shape=shapes,
        in_specs=[anywhere] * 5,
        out_specs=(
            pl.BlockSpec(memory_space=pltpu.VMEM),
            anywhere,
            pl.BlockSpec(memory_space=pltpu.VMEM),
        ),
        scratch_shapes=[
            pltpu.VMEM((16, 256, 512), BF16),
            pltpu.VMEM((16, 256, 512), BF16),
            pltpu.VMEM((128, 8192), BF16),
            pltpu.VMEM((8, 2, 2, 256, 128), BF16),
            pltpu.VMEM((256, 4096), BF16),
            pltpu.VMEM((8, 128, 512), BF16),
            pltpu.VMEM((8, 2, 64, 1024), BF16),
            pltpu.VMEM((4, 128, 512), F32),
            pltpu.VMEM((8, 128, 512), BF16),
            pltpu.VMEM((8, 3, 32, 512), BF16),
            pltpu.VMEM((7, 32, 512), BF16),
            pltpu.VMEM((7, 32, 512), BF16),
            pltpu.VMEM((256, 512), BF16),
            pltpu.VMEM((16, 256, 256), BF16),
            pltpu.VMEM((256, 512), F32),
            pltpu.VMEM((128, 512), F32),
            pltpu.VMEM((256, 512), jnp.int32),
            pltpu.VMEM((4, 256), F32),
            dma((4,)),
            dma, dma, dma,
            dma, dma((8,)),
            dma, dma((8,)),
            dma, dma((4, 2, 2)),
            dma, dma((4, 2, 2)),
            dma,
            dma, dma((8, 2)),
            dma, dma, dma,
            dma, dma((8,)),
            dma, dma((7,)),
            dma, dma,
            dma, dma,
        ],
        compiler_params=pltpu.CompilerParams(
            collective_id=0, has_side_effects=True, vmem_limit_bytes=62 << 20
        ),
        cost_estimate=pl.CostEstimate(
            flops=6 * 128 * 8192 * 512, bytes_accessed=24 << 20, transcendentals=0
        ),
    )(tokens, cotangent, base_copy, codes, scales.T)
    return pl.pallas_call(
        finish,
        out_shape=shapes,
        in_specs=[anywhere] * 3,
        out_specs=(anywhere,) * 3,
        scratch_shapes=[
            pltpu.VMEM((128, 512), BF16),
            pltpu.VMEM((128, 8192), BF16),
            pltpu.VMEM((256, 512), F32),
            dma((6,)),
            dma((6,)),
        ],
        compiler_params=pltpu.CompilerParams(vmem_limit_bytes=62 << 20),
    )(*results)


def solution(mesh):
    return jax.shard_map(
        body,
        mesh=mesh,
        in_specs=(
            P(("replica", "shard"), None),
            P(("replica", "shard"), None),
            P(),
            P("shard", None),
            P("shard", None),
        ),
        out_specs=(P(("replica", "shard"), None), P(("replica", "shard"), None), P("shard", None)),
        check_vma=False,
    )
```

```python
import math

import jax
import jax.numpy as jnp
from jax import lax
from jax.experimental import pallas as pl
from jax.experimental.pallas import tpu as pltpu
from jax.sharding import PartitionSpec as P

BF16 = jnp.bfloat16
F32 = jnp.float32


def kernel(
    tok, cot, base, codes, scales,
    proj, igrad, wgrad,
    W, BASE, TOK, TT, TK, CA, TW, GF, GX, XR, ZS, ZR, RR, IG, PA, PR, PJ, CO, SC,
    ld, tk_l, tk_s, tk_r, ca_s, ca_r, tw_s, tw_r, az_s, az_r, bz_s, bz_r, ao_s, ax_s, ax_r,
    ig_l, ig_s, ig_r, gx_s, gx_r, zs_s, zs_r, rr_s, rr_r, pa_s, pa_r,
):
    r = lax.axis_index("replica")
    s = lax.axis_index("shard")
    X, y = r // 4, r % 4
    l, z, c = s // 16, (s % 16) // 2, s % 2
    oc = 1 - c

    def dev(X=X, y=y, l=l, z=z, c=c):
        return {"replica": X * 4 + y, "shard": l * 16 + z * 2 + c}

    up, down = dev(z=(z + 1) % 8), dev(z=(z + 7) % 8)
    A, B, O = dev(l=1 - l), dev(X=1 - X, l=1 - l), dev(X=1 - X)
    peer = dev(c=oc)

    def wait(ref, sem):
        pltpu.make_async_copy(ref, ref, sem).wait()

    def send(src, dst, ssem, rsem, to):
        pltpu.make_async_remote_copy(src, dst, ssem, rsem, device_id=to).start()

    barrier = pltpu.get_barrier_semaphore()
    peers = [dev(X=1 - X, y=(y + d) % 4) for d in (2, 1, 3)]
    peers += [dev(y=(y + d) % 4, c=cc) for d in (2, 1, 3) for cc in (c, oc)]
    peers += [up, down]
    peers += [O, A, B, peer]
    for d in peers:
        pl.semaphore_signal(barrier, 1, device_id=d)

    pltpu.make_async_copy(tok, TOK, ld.at[3]).start()
    pltpu.make_async_copy(codes, CO, ld.at[0]).start()
    pltpu.make_async_copy(scales, SC, ld.at[1]).start()
    me8 = y * 2 + c
    pltpu.make_async_copy(cot, CA.at[me8], ca_r.at[me8]).start()

    def col(block, core):
        return pl.multiple_of((block * 2 + core) * 256, 256)

    def zof(n):
        return lax.rem(z + jnp.where(n % 2 == 1, 8 - (7 - n) // 2, 4 - n // 2), 8)

    def turn(n):
        def one(q, _):
            p, cc = q // 2, q % 2
            lanes = pl.ds(col(p * 8 + zof(n), cc), 256)
            TT[n, cc, p] = TOK[:, lanes].T
            return 0

        lax.fori_loop(0, 4, one, 0)

    pl.semaphore_wait(barrier, len(peers))

    def half(block, h):
        return W.at[block, pl.ds(h * 128, 128)]

    def send_z(block, t, way, h):
        send(half(block, h), half(block, h), az_s, az_r.at[t, way, h], (up, down)[way])

    def few(block, h):
        return W.at[block, pl.ds(h * 128, 64)]

    def most(block, h):
        return W.at[block, pl.ds(h * 128 + 64, 64)]

    def send_few(block, t, way, h):
        send(few(block, h), few(block, h), bz_s, bz_r.at[t, way, h], (up, down)[way])

    def send_x(block, zz, h):
        send(most(block, h), most(block, h), ax_s, ax_r.at[zz, h], (A, B)[h])

    for d in (1, 3, 2):
        send(cot, CA.at[me8], ca_s, ca_r.at[me8], dev(y=(y + d) % 4))
    send(cot, CA.at[me8], ca_s, ca_r.at[me8], peer)

    def send_tokens(b, _):
        src = pl.ds(col(b, oc), 256)
        dst = pl.ds(pl.multiple_of(b * 256, 256), 256)
        send(tok.at[:, src], TK.at[pl.ds(c * 128, 128), dst], tk_s, tk_r, peer)
        return 0

    my_lanes = pl.ds(pl.multiple_of(me8 * 128, 128), 128)

    def send_part(n):
        dst = TW.at[n, :, :, my_lanes]
        for d in (1, 3, 2, 0):
            j = (y + d) % 4
            rows = pl.ds(pl.multiple_of(j * 64, 64), 64)
            for cc in (c, oc):
                src = TT.at[n, cc, :, rows]
                if d == 0 and cc is c:
                    pltpu.make_async_copy(src, dst, tw_r.at[n]).start()
                else:
                    send(src, dst, tw_s, tw_r.at[n], dev(y=j, c=cc))

    wait(CO, ld.at[0])
    wait(SC, ld.at[1])
    own = l * 8 + z
    by_row = SC[...].T
    for g in range(4):
        lanes = pl.ds(g * 128, 128)
        W[own, :, lanes] = (CO[:, lanes].astype(F32) * by_row[:, g : g + 1]).astype(BF16)
    for h in range(2):
        send(half(own, h), half(own, h), ao_s, ax_r.at[z, h], (A, B)[h])
        send_z(own, 0, 0, h)
        send_z(own, 0, 1, h)
    wait(TOK, ld.at[3])
    for n in range(4):
        turn(n)
        send_part(n)
    def load_block(b, _):
        rows = pl.ds(col(b, c), 256)
        pltpu.make_async_copy(base.at[rows], BASE.at[b], ld.at[2]).start()
        dst = pl.ds(pl.multiple_of(b * 256, 256), 256)
        pltpu.make_async_copy(
            tok.at[:, rows], TK.at[pl.ds(c * 128, 128), dst], tk_l
        ).start()
        return 0

    lax.fori_loop(0, 16, load_block, 0)
    lax.fori_loop(0, 16, send_tokens, 0)

    PA[...] = jnp.zeros_like(PA)
    wait(CA.at[me8], ca_r.at[me8])
    wait(CA.at[y * 2 + oc], ca_r.at[y * 2 + oc])
    wait(BASE, ld.at[2])
    half_tokens = TK.at[pl.ds(0, 128)]
    wait(half_tokens, tk_l)
    wait(half_tokens, tk_r)

    def offset(m):
        return jnp.where(m % 2 == 1, 8 - (m + 1) // 2, m // 2)

    def use_block(other, m):
        zz = lax.rem(z + offset(m), 8)
        block = (1 - l if other is True else l if other is False else jnp.where(other, 1 - l, l)) * 8 + zz

        def arrive():
            for h in range(2):
                wait(most(block, h), ax_r.at[zz, h])

        if other is True:
            arrive()
        elif other is not False:
            pl.when(jnp.logical_and(other, m > 0))(arrive)

        w = (BASE[block].astype(F32) + W[block].astype(F32)).astype(BF16)
        lanes = pl.ds(pl.multiple_of(block * 256, 256), 256)
        PA[...] += jnp.dot(TK[:, lanes], w, preferred_element_type=F32)
        both = CA[pl.ds(y * 2, 2)].reshape(256, 512)
        IG[block] = lax.dot_general(
            both, w, (((1,), (1,)), ((), ())), preferred_element_type=F32
        ).astype(BF16)
        out = igrad.at[:, pl.ds(col(block, c), 256)]
        mine = IG.at[block, pl.ds(pl.multiple_of(c * 128, 128), 128)]
        theirs = IG.at[block, pl.ds(pl.multiple_of(oc * 128, 128), 128)]
        send(theirs, out, ig_s, ig_r, peer)
        pltpu.make_async_copy(mine, out, ig_l).start()

    def x_rows(p, half_x):
        return pl.ds(pl.multiple_of(p * 64 + half_x * 32, 32), 32)

    def part(n):
        @pl.when(n == 0)
        def _():
            for d in (1, 3, 2):
                k = ((y + d) % 4) * 2 + c
                wait(CA.at[k], ca_r.at[k])
                send(CA.at[k], CA.at[k], ca_s, ca_r.at[k], peer)
            for d in (1, 3, 2):
                k = ((y + d) % 4) * 2 + oc
                wait(CA.at[k], ca_r.at[k])

        wait(TW.at[n], tw_r.at[n])
        GF[n % 4] = jnp.dot(
            TW[n].reshape(128, 1024), CA[...].reshape(1024, 512), preferred_element_type=F32
        )
        GX[n] = GF[n % 4].astype(BF16)
        send(GX.at[n, x_rows(l, 1 - X)], XR.at[n, 2], gx_s, gx_r.at[n], O)
        send(GX.at[n, x_rows(1 - l, X)], XR.at[n, 0], gx_s, gx_r.at[n], A)
        send(GX.at[n, x_rows(1 - l, 1 - X)], XR.at[n, 1], gx_s, gx_r.at[n], B)

    def x_sum(n):
        wait(XR.at[n], gx_r.at[n])
        total = GF[n % 4, x_rows(l, X), :]
        for q in range(3):
            total = total + XR[n, q].astype(F32)
        return total

    def x_stage(n, even):
        total = x_sum(n)

        def pass_on():
            wait(ZR.at[n - 2], zs_r.at[n - 2])
            ZS[n] = (total + ZR[n - 2].astype(F32)).astype(BF16)

        if isinstance(n, int):
            pass_on()
        else:
            pl.when(n >= 2)(pass_on)

            @pl.when(n < 2)
            def _():
                ZS[n] = total.astype(BF16)

        to = dev(z=(z + jnp.where(even, 1, 7)) % 8)
        send(ZS.at[n], ZR.at[n], zs_s, zs_r.at[n], to)

    beside = (1 - l) * 8 + z

    def around(t):
        return (0, lax.rem(z + 7 - t, 8)), (1, lax.rem(z + t + 1, 8))

    def goes_on(t, h, way):
        return jnp.logical_or(t < 2, jnp.logical_and(t == 2, h == way))

    def gather_half(t, h):
        for way, zz in around(t):
            block = l * 8 + zz

            @pl.when(jnp.logical_or(t < 3, h == way))
            def _():
                wait(half(block, h), az_r.at[t, way, h])
                pl.when(goes_on(t, h, way))(lambda: send_z(block, t + 1, way, h))
                send_x(block, zz, h)

    def gather_few(t):
        for h in range(2):
            for way, zz in around(t):
                block = (1 - l) * 8 + zz

                @pl.when(jnp.logical_or(t < 3, h == way))
                def _():
                    wait(few(block, h), bz_r.at[t, way, h])
                    pl.when(goes_on(t, h, way))(lambda: send_few(block, t + 1, way, h))

    for h in range(2):
        wait(half(beside, h), ax_r.at[z, h])
        send_few(beside, 0, 0, h)
        send_few(beside, 0, 1, h)

    def pick(n, table):
        value = jnp.int32(0)
        for at, v in table.items():
            value = jnp.where(n == at, v, value)
        return value

    def among(n, places):
        return sum((n == at).astype(jnp.int32) for at in places) > 0

    def step(n, _):
        @pl.when(among(n, H0))
        def _():
            gather_half(pick(n, H0), 0)

        @pl.when(among(n, H1))
        def _():
            gather_half(pick(n, H1), 1)

        @pl.when(among(n, FEW))
        def _():
            gather_few(pick(n, FEW))

        @pl.when(n < 4)
        def _():
            turn(n + 4)
            send_part(n + 4)

        other, first = among(n, (1, 2, 6)), pick(n, FIRST)

        def one(q, _):
            use_block(other, first + q)
            return 0

        lax.fori_loop(0, pick(n, COUNT), one, 0)
        part(n)

        @pl.when(n >= 2)
        def _():
            x_stage(n - 2, n % 2 == 0)

        return 0

    H0 = {0: 0, 2: 1, 4: 2}
    H1 = {0: 0, 3: 1, 5: 2}
    FEW = {1: 0, 3: 1, 6: 2}
    FIRST = {0: 0, 1: 0, 2: 1, 4: 3, 6: 3, 7: 5}
    COUNT = {0: 3, 1: 1, 2: 2, 4: 2, 6: 2, 7: 2}

    lax.fori_loop(0, 8, step, 0)

    for h in range(2):
        gather_half(jnp.int32(3), h)
    use_block(False, 7)
    x_stage(6, True)
    gather_few(3)
    use_block(True, 5)
    total = x_sum(7)
    for n in (5, 6):
        wait(ZR.at[n], zs_r.at[n])
        total = total + ZR[n].astype(F32)
    my_piece = pl.ds(pl.multiple_of((y * 2 + X) * 32, 32), 32)
    RR[my_piece, :] = (total * (1.0 / math.sqrt(32768.0))).astype(BF16)
    for XX in (1 - X, X):
        for d in (2, 1, 3, 0):
            if XX is X and d == 0:
                continue
            to = dev(X=XX, y=(y + d) % 4)
            send(RR.at[my_piece], RR.at[my_piece], rr_s, rr_r, to)

    use_block(True, 6)
    use_block(True, 7)
    send(PA.at[pl.ds(pl.multiple_of(oc * 128, 128), 128)], PR, pa_s, pa_r, peer)

    wait(PR, pa_r)
    PJ[...] = (PA[pl.ds(pl.multiple_of(c * 128, 128), 128), :] + PR[...]).astype(BF16)
    pltpu.make_async_copy(PJ, proj, ld.at[0]).start()

    wait(RR.at[pl.ds(0, 224)], rr_r)
    pltpu.make_async_copy(RR, wgrad, ld.at[1]).start()

    wait(half_tokens, tk_s)
    wait(CA.at[pl.ds(0, 7)], ca_s)
    wait(TW.at[:, :, :, pl.ds(0, 896)], tw_s)
    wait(W.at[pl.ds(0, 7)], az_s)
    wait(W.at[pl.ds(0, 7), pl.ds(0, 128)], bz_s)
    wait(W.at[0], ao_s)
    wait(W.at[pl.ds(0, 7), pl.ds(0, 128)], ax_s)
    wait(XR, gx_s)
    wait(PR, pa_s)

    wait(ZS, zs_s)
    wait(ZR, rr_s)
    wait(PJ, ld.at[0])
    wait(half_tokens, ig_s)
    wait(half_tokens, ig_l)
    wait(half_tokens, ig_r)
    wait(RR, ld.at[1])


def finish(p_in, i_in, w_in, p_out, i_out, w_out, p_buf, i_buf, w_half, w_buf, sem_in, sem_out):
    pieces = [(w_in, w_half, w_buf, w_out)]
    for n in range(4):
        rows = pl.ds(n * 32, 32)
        pieces.append((i_in.at[rows], i_buf.at[rows], i_buf.at[rows], i_out.at[rows]))
    pieces.append((p_in, p_buf, p_buf, p_out))
    loads = [
        pltpu.make_async_copy(src, buf, sem_in.at[n])
        for n, (src, buf, _, _) in enumerate(pieces)
    ]
    stores = [
        pltpu.make_async_copy(buf, dst, sem_out.at[n])
        for n, (_, _, buf, dst) in enumerate(pieces)
    ]
    for load in loads:
        load.start()
    for n, (load, store) in enumerate(zip(loads, stores)):
        load.wait()
        if n == 0:
            w_buf[...] = w_half[...].astype(F32)
        store.start()
    for store in stores:
        store.wait()


def body(tokens, cotangent, base_copy, codes, scales):
    dma = pltpu.SemaphoreType.DMA
    anywhere = pl.BlockSpec(memory_space=pl.ANY)
    def shapes(of_weight):
        return (
            jax.ShapeDtypeStruct((128, 512), BF16),
            jax.ShapeDtypeStruct((128, 8192), BF16),
            jax.ShapeDtypeStruct((256, 512), of_weight),
        )

    results = pl.pallas_call(
        kernel,
        out_shape=shapes(BF16),
        in_specs=[anywhere] * 5,
        out_specs=(anywhere,) * 3,
        scratch_shapes=[
            pltpu.VMEM((16, 256, 512), BF16),
            pltpu.VMEM((16, 256, 512), BF16),
            pltpu.VMEM((128, 8192), BF16),
            pltpu.VMEM((8, 2, 2, 256, 128), BF16),
            pltpu.VMEM((256, 4096), BF16),
            pltpu.VMEM((8, 128, 512), BF16),
            pltpu.VMEM((8, 2, 64, 1024), BF16),
            pltpu.VMEM((4, 128, 512), F32),
            pltpu.VMEM((8, 128, 512), BF16),
            pltpu.VMEM((8, 3, 32, 512), BF16),
            pltpu.VMEM((7, 32, 512), BF16),
            pltpu.VMEM((7, 32, 512), BF16),
            pltpu.VMEM((256, 512), BF16),
            pltpu.VMEM((16, 256, 256), BF16),
            pltpu.VMEM((256, 512), F32),
            pltpu.VMEM((128, 512), F32),
            pltpu.VMEM((128, 512), BF16),
            pltpu.VMEM((256, 512), jnp.int32),
            pltpu.VMEM((4, 256), F32),
            dma((4,)),
            dma, dma, dma,
            dma, dma((8,)),
            dma, dma((8,)),
            dma, dma((4, 2, 2)),
            dma, dma((4, 2, 2)),
            dma,
            dma, dma((8, 2)),
            dma, dma, dma,
            dma, dma((8,)),
            dma, dma((7,)),
            dma, dma,
            dma, dma,
        ],
        compiler_params=pltpu.CompilerParams(
            collective_id=0, has_side_effects=True, vmem_limit_bytes=62 << 20
        ),
        cost_estimate=pl.CostEstimate(
            flops=6 * 128 * 8192 * 512, bytes_accessed=24 << 20, transcendentals=0
        ),
    )(tokens, cotangent, base_copy, codes, scales.T)
    return pl.pallas_call(
        finish,
        out_shape=shapes(F32),
        in_specs=[anywhere] * 3,
        out_specs=(anywhere,) * 3,
        scratch_shapes=[
            pltpu.VMEM((128, 512), BF16),
            pltpu.VMEM((128, 8192), BF16),
            pltpu.VMEM((256, 512), BF16),
            pltpu.VMEM((256, 512), F32),
            dma((6,)),
            dma((6,)),
        ],
        compiler_params=pltpu.CompilerParams(vmem_limit_bytes=62 << 20),
    )(*results)


def solution(mesh):
    return jax.shard_map(
        body,
        mesh=mesh,
        in_specs=(
            P(("replica", "shard"), None),
            P(("replica", "shard"), None),
            P(),
            P("shard", None),
            P("shard", None),
        ),
        out_specs=(P(("replica", "shard"), None), P(("replica", "shard"), None), P("shard", None)),
        check_vma=False,
    )
```

```python
import math

import jax
import jax.numpy as jnp
from jax import lax
from jax.experimental import pallas as pl
from jax.experimental.pallas import tpu as pltpu
from jax.sharding import PartitionSpec as P

BF16 = jnp.bfloat16
F32 = jnp.float32


def kernel(
    tok, cot, base, codes, scales,
    proj, igrad, wgrad,
    W, BASE, TOK, TT, TK, CA, TW, GF, GX, XR, ZS, ZR, RR, IG, PA, PR, PJ, CO, SC,
    ld, tk_l, tk_s, tk_r, ca_s, ca_r, tw_s, tw_r, az_s, az_r, bz_s, bz_r, ao_s, ax_s, ax_r,
    ig_l, ig_s, ig_r, gx_s, gx_r, zs_s, zs_r, rr_s, rr_r, pa_s, pa_r,
):
    r = lax.axis_index("replica")
    s = lax.axis_index("shard")
    X, y = r // 4, r % 4
    l, z, c = s // 16, (s % 16) // 2, s % 2
    oc = 1 - c

    def dev(X=X, y=y, l=l, z=z, c=c):
        return {"replica": X * 4 + y, "shard": l * 16 + z * 2 + c}

    up, down = dev(z=(z + 1) % 8), dev(z=(z + 7) % 8)
    A, B, O = dev(l=1 - l), dev(X=1 - X, l=1 - l), dev(X=1 - X)
    peer = dev(c=oc)

    def wait(ref, sem):
        pltpu.make_async_copy(ref, ref, sem).wait()

    def send(src, dst, ssem, rsem, to):
        pltpu.make_async_remote_copy(src, dst, ssem, rsem, device_id=to).start()

    barrier = pltpu.get_barrier_semaphore()
    peers = [dev(X=1 - X, y=(y + d) % 4) for d in (2, 1, 3)]
    peers += [dev(y=(y + d) % 4, c=cc) for d in (2, 1, 3) for cc in (c, oc)]
    peers += [up, down]
    peers += [O, A, B, peer]
    for d in peers:
        pl.semaphore_signal(barrier, 1, device_id=d)

    pltpu.make_async_copy(tok, TOK, ld.at[3]).start()
    pltpu.make_async_copy(codes, CO, ld.at[0]).start()
    pltpu.make_async_copy(scales, SC, ld.at[1]).start()
    me8 = y * 2 + c
    pltpu.make_async_copy(cot, CA.at[me8], ca_r.at[me8]).start()

    def col(block, core):
        return pl.multiple_of((block * 2 + core) * 256, 256)

    def zof(n):
        return lax.rem(z + jnp.where(n % 2 == 1, 8 - (7 - n) // 2, 4 - n // 2), 8)

    def turn(n):
        def one(q, _):
            p, cc = q // 2, q % 2
            lanes = pl.ds(col(p * 8 + zof(n), cc), 256)
            TT[n, cc, p] = TOK[:, lanes].T
            return 0

        lax.fori_loop(0, 4, one, 0)

    pl.semaphore_wait(barrier, len(peers))

    def half(block, h):
        return W.at[block, pl.ds(h * 128, 128)]

    def send_z(block, t, way, h):
        send(half(block, h), half(block, h), az_s, az_r.at[t, way, h], (up, down)[way])

    def few(block, h):
        return W.at[block, pl.ds(h * 128, 64)]

    def most(block, h):
        return W.at[block, pl.ds(h * 128 + 64, 64)]

    def send_few(block, t, way, h):
        send(few(block, h), few(block, h), bz_s, bz_r.at[t, way, h], (up, down)[way])

    def send_x(block, zz, h):
        send(most(block, h), most(block, h), ax_s, ax_r.at[zz, h], (A, B)[h])

    for d in (1, 3, 2):
        send(cot, CA.at[me8], ca_s, ca_r.at[me8], dev(y=(y + d) % 4))
    send(cot, CA.at[me8], ca_s, ca_r.at[me8], peer)

    def send_tokens(b, _):
        src = pl.ds(col(b, oc), 256)
        dst = pl.ds(pl.multiple_of(b * 256, 256), 256)
        send(tok.at[:, src], TK.at[pl.ds(c * 128, 128), dst], tk_s, tk_r, peer)
        return 0

    my_lanes = pl.ds(pl.multiple_of(me8 * 128, 128), 128)

    def send_part(n):
        dst = TW.at[n, :, :, my_lanes]
        for d in (1, 3, 2, 0):
            j = (y + d) % 4
            rows = pl.ds(pl.multiple_of(j * 64, 64), 64)
            for cc in (c, oc):
                src = TT.at[n, cc, :, rows]
                if d == 0 and cc is c:
                    pltpu.make_async_copy(src, dst, tw_r.at[n]).start()
                else:
                    send(src, dst, tw_s, tw_r.at[n], dev(y=j, c=cc))

    wait(CO, ld.at[0])
    wait(SC, ld.at[1])
    own = l * 8 + z
    by_row = SC[...].T
    for g in range(4):
        lanes = pl.ds(g * 128, 128)
        W[own, :, lanes] = (CO[:, lanes].astype(F32) * by_row[:, g : g + 1]).astype(BF16)
    for h in range(2):
        send(half(own, h), half(own, h), ao_s, ax_r.at[z, h], (A, B)[h])
        send_z(own, 0, 0, h)
        send_z(own, 0, 1, h)
    wait(TOK, ld.at[3])
    for n in range(4):
        turn(n)
        send_part(n)
    def load_block(b, _):
        rows = pl.ds(col(b, c), 256)
        pltpu.make_async_copy(base.at[rows], BASE.at[b], ld.at[2]).start()
        dst = pl.ds(pl.multiple_of(b * 256, 256), 256)
        pltpu.make_async_copy(
            tok.at[:, rows], TK.at[pl.ds(c * 128, 128), dst], tk_l
        ).start()
        return 0

    lax.fori_loop(0, 16, load_block, 0)
    lax.fori_loop(0, 16, send_tokens, 0)

    PA[...] = jnp.zeros_like(PA)
    wait(CA.at[me8], ca_r.at[me8])
    wait(CA.at[y * 2 + oc], ca_r.at[y * 2 + oc])
    wait(BASE, ld.at[2])
    half_tokens = TK.at[pl.ds(0, 128)]
    wait(half_tokens, tk_l)
    wait(half_tokens, tk_r)

    def offset(m):
        return jnp.where(m % 2 == 1, 8 - (m + 1) // 2, m // 2)

    def use_block(other, m):
        zz = lax.rem(z + offset(m), 8)
        block = (1 - l if other is True else l if other is False else jnp.where(other, 1 - l, l)) * 8 + zz

        def arrive():
            for h in range(2):
                wait(most(block, h), ax_r.at[zz, h])

        if other is True:
            arrive()
        elif other is not False:
            pl.when(jnp.logical_and(other, m > 0))(arrive)

        w = (BASE[block].astype(F32) + W[block].astype(F32)).astype(BF16)
        lanes = pl.ds(pl.multiple_of(block * 256, 256), 256)
        PA[...] += jnp.dot(TK[:, lanes], w, preferred_element_type=F32)
        both = CA[pl.ds(y * 2, 2)].reshape(256, 512)
        IG[block] = lax.dot_general(
            both, w, (((1,), (1,)), ((), ())), preferred_element_type=F32
        ).astype(BF16)
        out = igrad.at[:, pl.ds(col(block, c), 256)]
        mine = IG.at[block, pl.ds(pl.multiple_of(c * 128, 128), 128)]
        theirs = IG.at[block, pl.ds(pl.multiple_of(oc * 128, 128), 128)]
        send(theirs, out, ig_s, ig_r, peer)
        pltpu.make_async_copy(mine, out, ig_l).start()

    def x_rows(p, half_x):
        return pl.ds(pl.multiple_of(p * 64 + half_x * 32, 32), 32)

    def part(n):
        @pl.when(n == 0)
        def _():
            for d in (1, 3, 2):
                k = ((y + d) % 4) * 2 + c
                wait(CA.at[k], ca_r.at[k])
                send(CA.at[k], CA.at[k], ca_s, ca_r.at[k], peer)
            for d in (1, 3, 2):
                k = ((y + d) % 4) * 2 + oc
                wait(CA.at[k], ca_r.at[k])

        wait(TW.at[n], tw_r.at[n])
        GF[n % 4] = jnp.dot(
            TW[n].reshape(128, 1024), CA[...].reshape(1024, 512), preferred_element_type=F32
        )
        GX[n] = GF[n % 4].astype(BF16)
        send(GX.at[n, x_rows(l, 1 - X)], XR.at[n, 2], gx_s, gx_r.at[n], O)
        send(GX.at[n, x_rows(1 - l, X)], XR.at[n, 0], gx_s, gx_r.at[n], A)
        send(GX.at[n, x_rows(1 - l, 1 - X)], XR.at[n, 1], gx_s, gx_r.at[n], B)

    def x_sum(n):
        wait(XR.at[n], gx_r.at[n])
        total = GF[n % 4, x_rows(l, X), :]
        for q in range(3):
            total = total + XR[n, q].astype(F32)
        return total

    def x_stage(n, even):
        total = x_sum(n)

        def pass_on():
            wait(ZR.at[n - 2], zs_r.at[n - 2])
            ZS[n] = (total + ZR[n - 2].astype(F32)).astype(BF16)

        if isinstance(n, int):
            pass_on()
        else:
            pl.when(n >= 2)(pass_on)

            @pl.when(n < 2)
            def _():
                ZS[n] = total.astype(BF16)

        to = dev(z=(z + jnp.where(even, 1, 7)) % 8)
        send(ZS.at[n], ZR.at[n], zs_s, zs_r.at[n], to)

    beside = (1 - l) * 8 + z

    def around(t):
        return (0, lax.rem(z + 7 - t, 8)), (1, lax.rem(z + t + 1, 8))

    def goes_on(t, h, way):
        return jnp.logical_or(t < 2, jnp.logical_and(t == 2, h == way))

    def gather_half(t, h):
        for way, zz in around(t):
            block = l * 8 + zz

            @pl.when(jnp.logical_or(t < 3, h == way))
            def _():
                wait(half(block, h), az_r.at[t, way, h])
                pl.when(goes_on(t, h, way))(lambda: send_z(block, t + 1, way, h))
                send_x(block, zz, h)

    def gather_few(t):
        for h in range(2):
            for way, zz in around(t):
                block = (1 - l) * 8 + zz

                @pl.when(jnp.logical_or(t < 3, h == way))
                def _():
                    wait(few(block, h), bz_r.at[t, way, h])
                    pl.when(goes_on(t, h, way))(lambda: send_few(block, t + 1, way, h))

    for h in range(2):
        wait(half(beside, h), ax_r.at[z, h])
        send_few(beside, 0, 0, h)
        send_few(beside, 0, 1, h)

    def pick(n, table):
        value = jnp.int32(0)
        for at, v in table.items():
            value = jnp.where(n == at, v, value)
        return value

    def among(n, places):
        return sum((n == at).astype(jnp.int32) for at in places) > 0

    def step(n, _):
        @pl.when(among(n, H0))
        def _():
            gather_half(pick(n, H0), 0)

        @pl.when(among(n, H1))
        def _():
            gather_half(pick(n, H1), 1)

        @pl.when(among(n, FEW))
        def _():
            gather_few(pick(n, FEW))

        @pl.when(n < 4)
        def _():
            turn(n + 4)
            send_part(n + 4)

        other, first = among(n, (1, 2, 6)), pick(n, FIRST)

        def one(q, _):
            use_block(other, first + q)
            return 0

        lax.fori_loop(0, pick(n, COUNT), one, 0)
        part(n)

        @pl.when(n >= 2)
        def _():
            x_stage(n - 2, n % 2 == 0)

        return 0

    H0 = {0: 0, 2: 1, 4: 2}
    H1 = {0: 0, 3: 1, 5: 2}
    FEW = {1: 0, 4: 1, 7: 2}
    FIRST = {0: 0, 1: 0, 2: 1, 4: 3, 6: 3, 7: 5}
    COUNT = {0: 3, 1: 1, 2: 2, 4: 2, 6: 2, 7: 2}

    lax.fori_loop(0, 8, step, 0)

    for h in range(2):
        gather_half(jnp.int32(3), h)
    use_block(False, 7)
    x_stage(6, True)
    gather_few(3)
    use_block(True, 5)
    total = x_sum(7)
    for n in (5, 6):
        wait(ZR.at[n], zs_r.at[n])
        total = total + ZR[n].astype(F32)
    my_piece = pl.ds(pl.multiple_of((y * 2 + X) * 32, 32), 32)
    RR[my_piece, :] = (total * (1.0 / math.sqrt(32768.0))).astype(BF16)
    for XX in (1 - X, X):
        for d in (2, 1, 3, 0):
            if XX is X and d == 0:
                continue
            to = dev(X=XX, y=(y + d) % 4)
            send(RR.at[my_piece], RR.at[my_piece], rr_s, rr_r, to)

    use_block(True, 6)
    use_block(True, 7)
    send(PA.at[pl.ds(pl.multiple_of(oc * 128, 128), 128)], PR, pa_s, pa_r, peer)

    wait(PR, pa_r)
    PJ[...] = (PA[pl.ds(pl.multiple_of(c * 128, 128), 128), :] + PR[...]).astype(BF16)
    pltpu.make_async_copy(PJ, proj, ld.at[0]).start()

    wait(RR.at[pl.ds(0, 224)], rr_r)
    pltpu.make_async_copy(RR, wgrad, ld.at[1]).start()

    wait(half_tokens, tk_s)
    wait(CA.at[pl.ds(0, 7)], ca_s)
    wait(TW.at[:, :, :, pl.ds(0, 896)], tw_s)
    wait(W.at[pl.ds(0, 7)], az_s)
    wait(W.at[pl.ds(0, 7), pl.ds(0, 128)], bz_s)
    wait(W.at[0], ao_s)
    wait(W.at[pl.ds(0, 7), pl.ds(0, 128)], ax_s)
    wait(XR, gx_s)
    wait(PR, pa_s)

    wait(ZS, zs_s)
    wait(ZR, rr_s)
    wait(PJ, ld.at[0])
    wait(half_tokens, ig_s)
    wait(half_tokens, ig_l)
    wait(half_tokens, ig_r)
    wait(RR, ld.at[1])


def finish(p_in, i_in, w_in, p_out, i_out, w_out, p_buf, i_buf, w_half, w_buf, sem_in, sem_out):
    pieces = [(w_in, w_half, w_buf, w_out)]
    for n in range(4):
        rows = pl.ds(n * 32, 32)
        pieces.append((i_in.at[rows], i_buf.at[rows], i_buf.at[rows], i_out.at[rows]))
    pieces.append((p_in, p_buf, p_buf, p_out))
    loads = [
        pltpu.make_async_copy(src, buf, sem_in.at[n])
        for n, (src, buf, _, _) in enumerate(pieces)
    ]
    stores = [
        pltpu.make_async_copy(buf, dst, sem_out.at[n])
        for n, (_, _, buf, dst) in enumerate(pieces)
    ]
    for load in loads:
        load.start()
    for n, (load, store) in enumerate(zip(loads, stores)):
        load.wait()
        if n == 0:
            w_buf[...] = w_half[...].astype(F32)
        store.start()
    for store in stores:
        store.wait()


def body(tokens, cotangent, base_copy, codes, scales):
    dma = pltpu.SemaphoreType.DMA
    anywhere = pl.BlockSpec(memory_space=pl.ANY)
    def shapes(of_weight):
        return (
            jax.ShapeDtypeStruct((128, 512), BF16),
            jax.ShapeDtypeStruct((128, 8192), BF16),
            jax.ShapeDtypeStruct((256, 512), of_weight),
        )

    results = pl.pallas_call(
        kernel,
        out_shape=shapes(BF16),
        in_specs=[anywhere] * 5,
        out_specs=(anywhere,) * 3,
        scratch_shapes=[
            pltpu.VMEM((16, 256, 512), BF16),
            pltpu.VMEM((16, 256, 512), BF16),
            pltpu.VMEM((128, 8192), BF16),
            pltpu.VMEM((8, 2, 2, 256, 128), BF16),
            pltpu.VMEM((256, 4096), BF16),
            pltpu.VMEM((8, 128, 512), BF16),
            pltpu.VMEM((8, 2, 64, 1024), BF16),
            pltpu.VMEM((4, 128, 512), F32),
            pltpu.VMEM((8, 128, 512), BF16),
            pltpu.VMEM((8, 3, 32, 512), BF16),
            pltpu.VMEM((7, 32, 512), BF16),
            pltpu.VMEM((7, 32, 512), BF16),
            pltpu.VMEM((256, 512), BF16),
            pltpu.VMEM((16, 256, 256), BF16),
            pltpu.VMEM((256, 512), F32),
            pltpu.VMEM((128, 512), F32),
            pltpu.VMEM((128, 512), BF16),
            pltpu.VMEM((256, 512), jnp.int32),
            pltpu.VMEM((4, 256), F32),
            dma((4,)),
            dma, dma, dma,
            dma, dma((8,)),
            dma, dma((8,)),
            dma, dma((4, 2, 2)),
            dma, dma((4, 2, 2)),
            dma,
            dma, dma((8, 2)),
            dma, dma, dma,
            dma, dma((8,)),
            dma, dma((7,)),
            dma, dma,
            dma, dma,
        ],
        compiler_params=pltpu.CompilerParams(
            collective_id=0, has_side_effects=True, vmem_limit_bytes=62 << 20
        ),
        cost_estimate=pl.CostEstimate(
            flops=6 * 128 * 8192 * 512, bytes_accessed=24 << 20, transcendentals=0
        ),
    )(tokens, cotangent, base_copy, codes, scales.T)
    return pl.pallas_call(
        finish,
        out_shape=shapes(F32),
        in_specs=[anywhere] * 3,
        out_specs=(anywhere,) * 3,
        scratch_shapes=[
            pltpu.VMEM((128, 512), BF16),
            pltpu.VMEM((128, 8192), BF16),
            pltpu.VMEM((256, 512), BF16),
            pltpu.VMEM((256, 512), F32),
            dma((6,)),
            dma((6,)),
        ],
        compiler_params=pltpu.CompilerParams(vmem_limit_bytes=62 << 20),
    )(*results)


def solution(mesh):
    return jax.shard_map(
        body,
        mesh=mesh,
        in_specs=(
            P(("replica", "shard"), None),
            P(("replica", "shard"), None),
            P(),
            P("shard", None),
            P("shard", None),
        ),
        out_specs=(P(("replica", "shard"), None), P(("replica", "shard"), None), P("shard", None)),
        check_vma=False,
    )
```

```python
import math

import jax
import jax.numpy as jnp
from jax import lax
from jax.experimental import pallas as pl
from jax.experimental.pallas import tpu as pltpu
from jax.sharding import PartitionSpec as P

BF16 = jnp.bfloat16
F32 = jnp.float32


def kernel(
    tok, cot, base, codes, scales,
    proj, igrad, wgrad,
    W, BASE, TOK, TT, TK, CA, TW, GF, GX, XR, ZS, ZR, RR, IG, PA, PR, PJ, CO, SC,
    ld, tk_l, tk_s, tk_r, ca_s, ca_r, tw_s, tw_r, az_s, az_r, bz_s, bz_r, ao_s, ax_s, ax_r,
    ig_l, ig_s, ig_r, gx_s, gx_r, zs_s, zs_r, rr_s, rr_r, pa_s, pa_r,
):
    r = lax.axis_index("replica")
    s = lax.axis_index("shard")
    X, y = r // 4, r % 4
    l, z, c = s // 16, (s % 16) // 2, s % 2
    oc = 1 - c

    def dev(X=X, y=y, l=l, z=z, c=c):
        return {"replica": X * 4 + y, "shard": l * 16 + z * 2 + c}

    up, down = dev(z=(z + 1) % 8), dev(z=(z + 7) % 8)
    A, B, O = dev(l=1 - l), dev(X=1 - X, l=1 - l), dev(X=1 - X)
    peer = dev(c=oc)

    def wait(ref, sem):
        pltpu.make_async_copy(ref, ref, sem).wait()

    def send(src, dst, ssem, rsem, to):
        pltpu.make_async_remote_copy(src, dst, ssem, rsem, device_id=to).start()

    barrier = pltpu.get_barrier_semaphore()
    peers = [dev(X=1 - X, y=(y + d) % 4) for d in (2, 1, 3)]
    peers += [dev(y=(y + d) % 4, c=cc) for d in (2, 1, 3) for cc in (c, oc)]
    peers += [up, down]
    peers += [O, A, B, peer]
    for d in peers:
        pl.semaphore_signal(barrier, 1, device_id=d)

    pltpu.make_async_copy(tok, TOK, ld.at[3]).start()
    pltpu.make_async_copy(codes, CO, ld.at[0]).start()
    pltpu.make_async_copy(scales, SC, ld.at[1]).start()
    me8 = y * 2 + c
    pltpu.make_async_copy(cot, CA.at[me8], ca_r.at[me8]).start()

    def col(block, core):
        return pl.multiple_of((block * 2 + core) * 256, 256)

    def zof(n):
        return lax.rem(z + jnp.where(n % 2 == 1, 8 - (7 - n) // 2, 4 - n // 2), 8)

    def turn(n):
        def one(q, _):
            p, cc = q // 2, q % 2
            lanes = pl.ds(col(p * 8 + zof(n), cc), 256)
            TT[n, cc, p] = TOK[:, lanes].T
            return 0

        lax.fori_loop(0, 4, one, 0)

    pl.semaphore_wait(barrier, len(peers))

    def half(block, h):
        return W.at[block, pl.ds(h * 128, 128)]

    def send_z(block, t, way, h):
        send(half(block, h), half(block, h), az_s, az_r.at[t, way, h], (up, down)[way])

    def few(block, h):
        return W.at[block, pl.ds(h * 128, 64)]

    def most(block, h):
        return W.at[block, pl.ds(h * 128 + 64, 64)]

    def send_few(block, t, way, h):
        send(few(block, h), few(block, h), bz_s, bz_r.at[t, way, h], (up, down)[way])

    def send_x(block, zz, h):
        send(most(block, h), most(block, h), ax_s, ax_r.at[zz, h], (A, B)[h])

    for d in (1, 3, 2):
        send(cot, CA.at[me8], ca_s, ca_r.at[me8], dev(y=(y + d) % 4))
    send(cot, CA.at[me8], ca_s, ca_r.at[me8], peer)

    def send_tokens(b, _):
        src = pl.ds(col(b, oc), 256)
        dst = pl.ds(pl.multiple_of(b * 256, 256), 256)
        send(tok.at[:, src], TK.at[pl.ds(c * 128, 128), dst], tk_s, tk_r, peer)
        return 0

    my_lanes = pl.ds(pl.multiple_of(me8 * 128, 128), 128)

    def send_part(n):
        dst = TW.at[n, :, :, my_lanes]
        for d in (1, 3, 2, 0):
            j = (y + d) % 4
            rows = pl.ds(pl.multiple_of(j * 64, 64), 64)
            for cc in (c, oc):
                src = TT.at[n, cc, :, rows]
                if d == 0 and cc is c:
                    pltpu.make_async_copy(src, dst, tw_r.at[n]).start()
                else:
                    send(src, dst, tw_s, tw_r.at[n], dev(y=j, c=cc))

    wait(CO, ld.at[0])
    wait(SC, ld.at[1])
    own = l * 8 + z
    by_row = SC[...].T
    for g in range(4):
        lanes = pl.ds(g * 128, 128)
        W[own, :, lanes] = (CO[:, lanes].astype(F32) * by_row[:, g : g + 1]).astype(BF16)
    for h in range(2):
        send(half(own, h), half(own, h), ao_s, ax_r.at[z, h], (A, B)[h])
        send_z(own, 0, 0, h)
        send_z(own, 0, 1, h)
    wait(TOK, ld.at[3])
    for n in range(4):
        turn(n)
        send_part(n)
    def load_block(b, _):
        rows = pl.ds(col(b, c), 256)
        pltpu.make_async_copy(base.at[rows], BASE.at[b], ld.at[2]).start()
        dst = pl.ds(pl.multiple_of(b * 256, 256), 256)
        pltpu.make_async_copy(
            tok.at[:, rows], TK.at[pl.ds(c * 128, 128), dst], tk_l
        ).start()
        return 0

    lax.fori_loop(0, 16, load_block, 0)
    lax.fori_loop(0, 16, send_tokens, 0)

    PA[...] = jnp.zeros_like(PA)
    wait(CA.at[me8], ca_r.at[me8])
    wait(CA.at[y * 2 + oc], ca_r.at[y * 2 + oc])
    wait(BASE, ld.at[2])
    half_tokens = TK.at[pl.ds(0, 128)]
    wait(half_tokens, tk_l)
    wait(half_tokens, tk_r)

    def offset(m):
        return jnp.where(m % 2 == 1, 8 - (m + 1) // 2, m // 2)

    def use_block(other, m):
        zz = lax.rem(z + offset(m), 8)
        block = (1 - l if other is True else l if other is False else jnp.where(other, 1 - l, l)) * 8 + zz

        def arrive():
            for h in range(2):
                wait(most(block, h), ax_r.at[zz, h])

        if other is True:
            arrive()
        elif other is not False:
            pl.when(jnp.logical_and(other, m > 0))(arrive)

        w = (BASE[block].astype(F32) + W[block].astype(F32)).astype(BF16)
        lanes = pl.ds(pl.multiple_of(block * 256, 256), 256)
        PA[...] += jnp.dot(TK[:, lanes], w, preferred_element_type=F32)
        both = CA[pl.ds(y * 2, 2)].reshape(256, 512)
        IG[block] = lax.dot_general(
            both, w, (((1,), (1,)), ((), ())), preferred_element_type=F32
        ).astype(BF16)
        out = igrad.at[:, pl.ds(col(block, c), 256)]
        mine = IG.at[block, pl.ds(pl.multiple_of(c * 128, 128), 128)]
        theirs = IG.at[block, pl.ds(pl.multiple_of(oc * 128, 128), 128)]
        send(theirs, out, ig_s, ig_r, peer)
        pltpu.make_async_copy(mine, out, ig_l).start()

    def x_rows(p, half_x):
        return pl.ds(pl.multiple_of(p * 64 + half_x * 32, 32), 32)

    def part(n):
        @pl.when(n == 0)
        def _():
            for d in (1, 3, 2):
                k = ((y + d) % 4) * 2 + c
                wait(CA.at[k], ca_r.at[k])
                send(CA.at[k], CA.at[k], ca_s, ca_r.at[k], peer)
            for d in (1, 3, 2):
                k = ((y + d) % 4) * 2 + oc
                wait(CA.at[k], ca_r.at[k])

        wait(TW.at[n], tw_r.at[n])
        GF[n % 4] = jnp.dot(
            TW[n].reshape(128, 1024), CA[...].reshape(1024, 512), preferred_element_type=F32
        )
        GX[n] = GF[n % 4].astype(BF16)
        send(GX.at[n, x_rows(l, 1 - X)], XR.at[n, 2], gx_s, gx_r.at[n], O)
        send(GX.at[n, x_rows(1 - l, X)], XR.at[n, 0], gx_s, gx_r.at[n], A)
        send(GX.at[n, x_rows(1 - l, 1 - X)], XR.at[n, 1], gx_s, gx_r.at[n], B)

    def x_sum(n):
        wait(XR.at[n], gx_r.at[n])
        total = GF[n % 4, x_rows(l, X), :]
        for q in range(3):
            total = total + XR[n, q].astype(F32)
        return total

    def x_stage(n, even):
        total = x_sum(n)

        def pass_on():
            wait(ZR.at[n - 2], zs_r.at[n - 2])
            ZS[n] = (total + ZR[n - 2].astype(F32)).astype(BF16)

        if isinstance(n, int):
            pass_on()
        else:
            pl.when(n >= 2)(pass_on)

            @pl.when(n < 2)
            def _():
                ZS[n] = total.astype(BF16)

        to = dev(z=(z + jnp.where(even, 1, 7)) % 8)
        send(ZS.at[n], ZR.at[n], zs_s, zs_r.at[n], to)

    beside = (1 - l) * 8 + z

    def around(t):
        return (0, lax.rem(z + 7 - t, 8)), (1, lax.rem(z + t + 1, 8))

    def goes_on(t, h, way):
        return jnp.logical_or(t < 2, jnp.logical_and(t == 2, h == way))

    def gather_half(t, h):
        for way, zz in around(t):
            block = l * 8 + zz

            @pl.when(jnp.logical_or(t < 3, h == way))
            def _():
                wait(half(block, h), az_r.at[t, way, h])
                pl.when(goes_on(t, h, way))(lambda: send_z(block, t + 1, way, h))
                send_x(block, zz, h)

    def gather_few(t):
        for h in range(2):
            for way, zz in around(t):
                block = (1 - l) * 8 + zz

                @pl.when(jnp.logical_or(t < 3, h == way))
                def _():
                    wait(few(block, h), bz_r.at[t, way, h])
                    pl.when(goes_on(t, h, way))(lambda: send_few(block, t + 1, way, h))

    for h in range(2):
        wait(half(beside, h), ax_r.at[z, h])
        send_few(beside, 0, 0, h)
        send_few(beside, 0, 1, h)

    def pick(n, table):
        value = jnp.int32(0)
        for at, v in table.items():
            value = jnp.where(n == at, v, value)
        return value

    def among(n, places):
        return sum((n == at).astype(jnp.int32) for at in places) > 0

    def step(n, _):
        @pl.when(among(n, H0))
        def _():
            gather_half(pick(n, H0), 0)

        @pl.when(among(n, H1))
        def _():
            gather_half(pick(n, H1), 1)

        @pl.when(among(n, FEW))
        def _():
            gather_few(pick(n, FEW))

        @pl.when(n < 4)
        def _():
            turn(n + 4)
            send_part(n + 4)

        other, first = among(n, (1, 2, 6)), pick(n, FIRST)

        def one(q, _):
            use_block(other, first + q)
            return 0

        lax.fori_loop(0, pick(n, COUNT), one, 0)
        part(n)

        @pl.when(n >= 2)
        def _():
            x_stage(n - 2, n % 2 == 0)

        return 0

    H0 = {0: 0, 2: 1, 4: 2}
    H1 = {0: 0, 3: 1, 5: 2}
    FEW = {1: 0, 4: 1, 7: 2}
    FIRST = {0: 0, 1: 0, 2: 1, 4: 3, 6: 3, 7: 5}
    COUNT = {0: 3, 1: 1, 2: 2, 4: 2, 6: 2, 7: 2}

    lax.fori_loop(0, 8, step, 0)

    for h in range(2):
        gather_half(jnp.int32(3), h)
    use_block(False, 7)
    x_stage(6, True)
    gather_few(3)
    use_block(True, 5)
    total = x_sum(7)
    for n in (5, 6):
        wait(ZR.at[n], zs_r.at[n])
        total = total + ZR[n].astype(F32)
    my_piece = pl.ds(pl.multiple_of((y * 2 + X) * 32, 32), 32)
    RR[my_piece, :] = (total * (1.0 / math.sqrt(32768.0))).astype(BF16)
    for XX in (1 - X, X):
        for d in (2, 1, 3, 0):
            if XX is X and d == 0:
                continue
            to = dev(X=XX, y=(y + d) % 4)
            send(RR.at[my_piece], wgrad.at[my_piece], rr_s, rr_r, to)
    pltpu.make_async_copy(RR.at[my_piece], wgrad.at[my_piece], ld.at[1]).start()

    use_block(True, 6)
    use_block(True, 7)
    send(PA.at[pl.ds(pl.multiple_of(oc * 128, 128), 128)], PR, pa_s, pa_r, peer)

    wait(PR, pa_r)
    PJ[...] = (PA[pl.ds(pl.multiple_of(c * 128, 128), 128), :] + PR[...]).astype(BF16)
    pltpu.make_async_copy(PJ, proj, ld.at[0]).start()

    wait(half_tokens, tk_s)
    wait(CA.at[pl.ds(0, 7)], ca_s)
    wait(TW.at[:, :, :, pl.ds(0, 896)], tw_s)
    wait(W.at[pl.ds(0, 7)], az_s)
    wait(W.at[pl.ds(0, 7), pl.ds(0, 128)], bz_s)
    wait(W.at[0], ao_s)
    wait(W.at[pl.ds(0, 7), pl.ds(0, 128)], ax_s)
    wait(XR, gx_s)
    wait(PR, pa_s)

    wait(ZS, zs_s)
    wait(ZR, rr_s)
    wait(PJ, ld.at[0])
    wait(half_tokens, ig_s)
    wait(half_tokens, ig_l)
    wait(half_tokens, ig_r)
    wait(RR.at[my_piece], ld.at[1])
    wait(RR.at[pl.ds(0, 224)], rr_r)


def finish(p_in, i_in, w_in, p_out, i_out, w_out, p_buf, i_buf, w_half, w_buf, sem_in, sem_out):
    pieces = [(w_in, w_half, w_buf, w_out)]
    for n in range(4):
        rows = pl.ds(n * 32, 32)
        pieces.append((i_in.at[rows], i_buf.at[rows], i_buf.at[rows], i_out.at[rows]))
    pieces.append((p_in, p_buf, p_buf, p_out))
    loads = [
        pltpu.make_async_copy(src, buf, sem_in.at[n])
        for n, (src, buf, _, _) in enumerate(pieces)
    ]
    stores = [
        pltpu.make_async_copy(buf, dst, sem_out.at[n])
        for n, (_, _, buf, dst) in enumerate(pieces)
    ]
    for load in loads:
        load.start()
    for n, (load, store) in enumerate(zip(loads, stores)):
        load.wait()
        if n == 0:
            w_buf[...] = w_half[...].astype(F32)
        store.start()
    for store in stores:
        store.wait()


def body(tokens, cotangent, base_copy, codes, scales):
    dma = pltpu.SemaphoreType.DMA
    anywhere = pl.BlockSpec(memory_space=pl.ANY)
    def shapes(of_weight):
        return (
            jax.ShapeDtypeStruct((128, 512), BF16),
            jax.ShapeDtypeStruct((128, 8192), BF16),
            jax.ShapeDtypeStruct((256, 512), of_weight),
        )

    results = pl.pallas_call(
        kernel,
        out_shape=shapes(BF16),
        in_specs=[anywhere] * 5,
        out_specs=(anywhere,) * 3,
        scratch_shapes=[
            pltpu.VMEM((16, 256, 512), BF16),
            pltpu.VMEM((16, 256, 512), BF16),
            pltpu.VMEM((128, 8192), BF16),
            pltpu.VMEM((8, 2, 2, 256, 128), BF16),
            pltpu.VMEM((256, 4096), BF16),
            pltpu.VMEM((8, 128, 512), BF16),
            pltpu.VMEM((8, 2, 64, 1024), BF16),
            pltpu.VMEM((4, 128, 512), F32),
            pltpu.VMEM((8, 128, 512), BF16),
            pltpu.VMEM((8, 3, 32, 512), BF16),
            pltpu.VMEM((7, 32, 512), BF16),
            pltpu.VMEM((7, 32, 512), BF16),
            pltpu.VMEM((256, 512), BF16),
            pltpu.VMEM((16, 256, 256), BF16),
            pltpu.VMEM((256, 512), F32),
            pltpu.VMEM((128, 512), F32),
            pltpu.VMEM((128, 512), BF16),
            pltpu.VMEM((256, 512), jnp.int32),
            pltpu.VMEM((4, 256), F32),
            dma((4,)),
            dma, dma, dma,
            dma, dma((8,)),
            dma, dma((8,)),
            dma, dma((4, 2, 2)),
            dma, dma((4, 2, 2)),
            dma,
            dma, dma((8, 2)),
            dma, dma, dma,
            dma, dma((8,)),
            dma, dma((7,)),
            dma, dma,
            dma, dma,
        ],
        compiler_params=pltpu.CompilerParams(
            collective_id=0, has_side_effects=True, vmem_limit_bytes=62 << 20
        ),
        cost_estimate=pl.CostEstimate(
            flops=6 * 128 * 8192 * 512, bytes_accessed=24 << 20, transcendentals=0
        ),
    )(tokens, cotangent, base_copy, codes, scales.T)
    return pl.pallas_call(
        finish,
        out_shape=shapes(F32),
        in_specs=[anywhere] * 3,
        out_specs=(anywhere,) * 3,
        scratch_shapes=[
            pltpu.VMEM((128, 512), BF16),
            pltpu.VMEM((128, 8192), BF16),
            pltpu.VMEM((256, 512), BF16),
            pltpu.VMEM((256, 512), F32),
            dma((6,)),
            dma((6,)),
        ],
        compiler_params=pltpu.CompilerParams(vmem_limit_bytes=62 << 20),
    )(*results)


def solution(mesh):
    return jax.shard_map(
        body,
        mesh=mesh,
        in_specs=(
            P(("replica", "shard"), None),
            P(("replica", "shard"), None),
            P(),
            P("shard", None),
            P("shard", None),
        ),
        out_specs=(P(("replica", "shard"), None), P(("replica", "shard"), None), P("shard", None)),
        check_vma=False,
    )
```
